32 devices in a mesh: group: 4 (over z), peer: 8 (over y, x, core).
Axes of the slice: x: 2, y: 2, z: 4, core: 2. Of those that a mesh axis runs over, the one named last changes fastest.
Arguments:
- embed: bfloat16 [16384, 1024], P(('group', 'peer')), may hold values from -64 to 64
- lengths: int32 [4, 512], P('group'), may hold values from 0 to 8, as said below
- w_in: bfloat16 [1024, 2048], replicated, may hold values from -0.1875 to 0.1875
- w_out: bfloat16 [512, 1024], replicated, may hold values from -0.25 to 0.25
- cotangent: bfloat16 [8192, 1024], P(('group', 'peer')), may hold values from -6 to 6
Outputs:
- out_work: bfloat16 [8192, 1024], P(('group', 'peer'))
- grad_home: bfloat16 [16384, 1024], P(('group', 'peer'))
- grad_out_proj: float32 [512, 1024], P('peer', 'group')
The draws below stay inside these ranges and needn't reach their ends.
Inputs may be any that keep to these rules, and one draw needn't show every extreme that they name: `lengths`: in every group exactly 256 blocks are live, and some peer of every group has all 64 of its blocks live; some block of every group has length 8.
All inputs are finite; a program needn't handle non-finite values.
Results may differ from the reference program's by a relative error of at most 0.0087.
Values may be sent and summed in bfloat16 or wider, within the bound.
A program may use at most 64 MiB of HBM per device.

```python
import math
import jax
import jax.numpy as jnp
from jax import lax

D = 1024
HD = 128
HH = 512
BLK = 8
WB = 32
HB = 64
HOME_ROWS = 16384
WORK_ROWS = 8192
N_GROUP = 4
N_PEER = 8


def draw_embed(key, part):
    first, second, third = jax.random.split(key, 3)
    row_scale = jnp.exp(jax.random.uniform(first, (HOME_ROWS, 1), jnp.float32, math.log(0.32), math.log(3.2)))
    col_scale = jnp.exp(jax.random.uniform(second, (1, D), jnp.float32, math.log(0.32), math.log(3.2)))
    noise = jax.random.truncated_normal(third, -4.0, 4.0, (HOME_ROWS, D), jnp.float32)
    return (noise * row_scale * col_scale).astype(jnp.bfloat16)


def draw_lengths(key, part):

    def one_group(group_key):
        first, second, third, fourth = jax.random.split(group_key, 4)
        order = jax.random.permutation(first, N_PEER).astype(jnp.int32)
        half_count = N_PEER // 2
        delta = jax.random.randint(second, (half_count,), 0, WB + 1, jnp.int32)
        delta = delta.at[0].set(WB)
        counts = jnp.full((N_PEER,), WB, jnp.int32)
        counts = counts.at[order[:half_count]].add(delta)
        counts = counts.at[order[half_count:]].add(-delta)
        slot_keys = jax.random.split(third, N_PEER)
        slots = jax.vmap(lambda slot_key: jax.random.permutation(slot_key, HB))(slot_keys).astype(jnp.int32)
        is_live = slots < counts[:, None]
        event_counts = jax.random.randint(fourth, (N_PEER, HB), 1, BLK + 1, jnp.int32)
        busiest = order[0]
        event_counts = event_counts.at[busiest].set(jnp.where(slots[busiest] == 0, BLK, event_counts[busiest]))
        return jnp.where(is_live, event_counts, 0).reshape(-1).astype(jnp.int32)
    group_keys = jax.random.split(key, N_GROUP)
    return jax.vmap(one_group)(group_keys)


def steps_of(key, extent, cuts, smallest, largest):
    def one(dim, parts):
        heights = jax.random.uniform(jax.random.fold_in(jax.random.fold_in(key, 6), dim), (parts,), jnp.float32, smallest / len(cuts), largest / len(cuts))
        return jnp.repeat(jnp.exp(heights), extent[dim] // parts).reshape((-1,) + (1,) * (len(extent) - dim - 1))

    loudness = one(*cuts[0])
    for cut in cuts[1:]:
        loudness = loudness * one(*cut)
    return loudness


def normal_values(rng, extent, spread, most, shards=(), kind=jnp.bfloat16):
    entries = spread * jax.random.normal(rng, extent, jnp.float32)
    if shards:
        entries = entries * steps_of(rng, extent, shards, -0.22, 0.18)
    return jnp.clip(entries, -most, most).astype(kind)


def setup_inputs(seed: int = 0) -> dict:
    arg_keys = jax.random.split(jax.random.key(seed), 6)
    embed = draw_embed(jax.random.fold_in(arg_keys[5], 71), 0)
    lengths = draw_lengths(jax.random.fold_in(arg_keys[5], 71), 0)
    w_in = normal_values(arg_keys[2], (D, 4 * HH), D ** -0.5, 0.1875)
    w_out = normal_values(arg_keys[3], (HH, D), HH ** -0.5, 0.25)
    cotangent = normal_values(arg_keys[4], (WORK_ROWS, D), 1.0, 6.0, ((0, 32),))
    return dict(embed=embed, lengths=lengths, w_in=w_in, w_out=w_out, cotangent=cotangent)


EPSILON = 1e-06
MIX_FLOOR = 1.0

def plan_tables(block_lengths):
    block_total = block_lengths.shape[1]
    is_live = (block_lengths > 0).astype(jnp.int32)
    counts = lax.optimization_barrier(jnp.sum(is_live, axis=1)).astype(jnp.int32)
    prefix = (jnp.cumsum(counts) - counts).astype(jnp.int32)
    block_rank = (jnp.cumsum(is_live, axis=1) - is_live).astype(jnp.int32)
    slot_index = jnp.arange(block_total, dtype=jnp.int32)
    chosen = (block_rank[:, :, None] == slot_index[None, None, :]) & (is_live[:, :, None] > 0)
    chosen_int = chosen.astype(jnp.int32)
    block_of = lax.optimization_barrier(jnp.sum(chosen_int * slot_index[None, :, None], axis=1)).astype(jnp.int32)
    length_of = lax.optimization_barrier(jnp.sum(chosen_int * block_lengths[:, :, None], axis=1)).astype(jnp.int32)
    return (counts, prefix, block_rank, block_of, length_of)

def layer(inputs, work_len, w_in, w_out):
    block_count = inputs.shape[0]
    block_len = inputs.shape[1]
    model_width = inputs.shape[2]
    attn_width = w_out.shape[0]
    head_count = attn_width // HD
    floated = inputs.astype(jnp.float32)
    row_mean = lax.optimization_barrier(jnp.mean(floated, axis=-1, keepdims=True))
    centred = floated - row_mean
    row_var = lax.optimization_barrier(jnp.mean(centred * centred, axis=-1, keepdims=True))
    normed = (centred * lax.rsqrt(row_var + EPSILON)).astype(jnp.bfloat16)
    projected = jnp.dot(normed.reshape(-1, model_width), w_in, preferred_element_type=jnp.float32)
    activated = jax.nn.silu(projected).astype(jnp.bfloat16)
    gating = activated[:, :attn_width]
    values = activated[:, attn_width:2 * attn_width].reshape(block_count, block_len, head_count, HD)
    queries = activated[:, 2 * attn_width:3 * attn_width].reshape(block_count, block_len, head_count, HD)
    key_rows = activated[:, 3 * attn_width:].reshape(block_count, block_len, head_count, HD)
    scores = jnp.einsum('bihd,bjhd->bhij', queries.astype(jnp.float32), key_rows.astype(jnp.float32)) * HD ** (-0.5)
    position = jnp.arange(block_len, dtype=jnp.int32)
    causal = position[None, :] <= position[:, None]
    limit = work_len[:, None, None, None]
    allowed = causal[None, None, :, :] & (position[None, None, None, :] < limit) & (position[None, None, :, None] < limit)
    weights = jnp.where(allowed, jax.nn.silu(scores), 0.0).astype(jnp.bfloat16)
    mixed = jnp.einsum('bhij,bjhd->bihd', weights.astype(jnp.float32), values.astype(jnp.float32))
    mixed = mixed.reshape(block_count * block_len, attn_width)
    mix_mean = lax.optimization_barrier(jnp.mean(mixed, axis=-1, keepdims=True))
    mix_centred = mixed - mix_mean
    mix_var = lax.optimization_barrier(jnp.mean(mix_centred * mix_centred, axis=-1, keepdims=True))
    gated = (mix_centred * lax.rsqrt(jnp.maximum(mix_var, MIX_FLOOR)) * gating.astype(jnp.float32)).astype(jnp.bfloat16)
    output = floated.reshape(-1, model_width) + jnp.dot(gated, w_out, preferred_element_type=jnp.float32)
    rows_ok = (position[None, :] < work_len[:, None]).reshape(-1, 1)
    result = jnp.where(rows_ok, output, 0.0).astype(jnp.bfloat16).reshape(block_count, block_len, model_width)
    return (result, gated)

def reference(embed, lengths, w_in, w_out, cotangent):
    group_total = lengths.shape[0]
    peer_count = N_PEER
    home_rows = embed.reshape(group_total, peer_count * HB, BLK, D)
    cotan_rows = cotangent.reshape(group_total, peer_count * WB, BLK, D)

    def one_group(total_grad, inputs_group):
        group_rows, group_lengths, group_cotan = inputs_group
        block_lengths = group_lengths.reshape(peer_count, HB)
        counts, prefix, block_rank, block_of, length_of = plan_tables(block_lengths)
        slot_ids = jnp.arange(WB, dtype=jnp.int32)
        peer_ids = jnp.arange(peer_count, dtype=jnp.int32)
        ticket = (slot_ids[None, :] * peer_count + peer_ids[:, None]).reshape(-1)
        source_end = prefix + counts
        source = lax.optimization_barrier(jnp.sum((source_end[None, :] <= ticket[:, None]).astype(jnp.int32), axis=1)).astype(jnp.int32)
        source = jnp.minimum(source, peer_count - 1)
        within = jnp.clip(ticket - prefix[source], 0, HB - 1)
        home_index = source * HB + block_of[source, within]
        work_len = length_of[source, within]
        work_rows = group_rows[home_index]
        result, pullback, gated = jax.vjp(lambda inputs: layer(inputs, work_len, w_in, w_out), work_rows, has_aux=True)
        grad_work, = pullback(group_cotan)
        step_grad = lax.dot_general(gated, group_cotan.reshape(-1, D), (((0,), (0,)), ((), ())), preferred_element_type=jnp.float32)
        home_ticket = prefix[:, None] + block_rank
        work_position = home_ticket % peer_count * WB + home_ticket // peer_count
        work_position = jnp.clip(work_position, 0, peer_count * WB - 1).reshape(-1)
        is_live = (block_lengths > 0).reshape(-1)
        grad_back = jnp.where(is_live[:, None, None], grad_work[work_position], jnp.zeros((), jnp.bfloat16))
        return (total_grad + step_grad, (result, grad_back))
    start_grad = jnp.zeros((HH, D), jnp.float32)
    total_grad, (results, grads) = lax.scan(one_group, start_grad, (home_rows, lengths, cotan_rows))
    grad_scale = 1.0 / math.sqrt(WORK_ROWS)
    return (results.reshape(-1, D), grads.reshape(-1, D), total_grad * grad_scale)
```

```python
import functools
import math

import jax
import jax.numpy as jnp
from jax import lax
from jax.experimental import pallas as pl
from jax.experimental.pallas import tpu as pltpu
from jax.sharding import PartitionSpec as P

HD = 128
BLK = 8


EPSILON = 1e-06
MIX_FLOOR = 1.0


def shortened(shard):

    def short(part):
        return part.astype(jnp.bfloat16) if part.dtype == jnp.float32 else part

    return jax.tree.map(short, shard)


def plan_tables(block_lengths):
    block_total = block_lengths.shape[1]
    is_live = (block_lengths > 0).astype(jnp.int32)
    counts = jnp.sum(is_live, axis=1)
    prefix = jnp.cumsum(counts) - counts
    block_rank = jnp.cumsum(is_live, axis=1) - is_live
    slot_index = jnp.arange(block_total, dtype=jnp.int32)
    chosen = (block_rank[:, :, None] == slot_index[None, None, :]) & (is_live[:, :, None] > 0)
    chosen_int = chosen.astype(jnp.int32)
    block_of = jnp.sum(chosen_int * slot_index[None, :, None], axis=1)
    length_of = jnp.sum(chosen_int * block_lengths[:, :, None], axis=1)
    return (counts, prefix, block_rank, block_of, length_of)


def layer(inputs, work_len, w_in, w_out):
    block_count = inputs.shape[0]
    block_len = inputs.shape[1]
    model_width = inputs.shape[2]
    attn_width = w_out.shape[0]
    head_count = attn_width // HD
    floated = inputs.astype(jnp.float32)
    row_mean = jnp.mean(floated, axis=-1, keepdims=True)
    centred = floated - row_mean
    row_var = jnp.mean(centred * centred, axis=-1, keepdims=True)
    normed = (centred * lax.rsqrt(row_var + EPSILON)).astype(jnp.bfloat16)
    projected = jnp.dot(normed.reshape(-1, model_width), w_in, preferred_element_type=jnp.float32)
    activated = jax.nn.silu(projected).astype(jnp.bfloat16)
    gating = activated[:, :attn_width]
    values = activated[:, attn_width : 2 * attn_width].reshape(
        block_count, block_len, head_count, HD
    )
    queries = activated[:, 2 * attn_width : 3 * attn_width].reshape(
        block_count, block_len, head_count, HD
    )
    key_rows = activated[:, 3 * attn_width :].reshape(block_count, block_len, head_count, HD)
    scores = jnp.einsum(
        "bihd,bjhd->bhij", queries.astype(jnp.float32), key_rows.astype(jnp.float32)
    ) * HD ** (-0.5)
    position = jnp.arange(block_len, dtype=jnp.int32)
    causal = position[None, :] <= position[:, None]
    limit = work_len[:, None, None, None]
    allowed = (
        causal[None, None, :, :]
        & (position[None, None, None, :] < limit)
        & (position[None, None, :, None] < limit)
    )
    weights = jnp.where(allowed, jax.nn.silu(scores), 0.0).astype(jnp.bfloat16)
    mixed = jnp.einsum("bhij,bjhd->bihd", weights.astype(jnp.float32), values.astype(jnp.float32))
    mixed = mixed.reshape(block_count * block_len, attn_width)
    mix_mean = jnp.mean(mixed, axis=-1, keepdims=True)
    mix_centred = mixed - mix_mean
    mix_var = jnp.mean(mix_centred * mix_centred, axis=-1, keepdims=True)
    gated = (
        mix_centred * lax.rsqrt(jnp.maximum(mix_var, MIX_FLOOR)) * gating.astype(jnp.float32)
    ).astype(jnp.bfloat16)
    output = floated.reshape(-1, model_width) + jnp.dot(
        gated, w_out, preferred_element_type=jnp.float32
    )
    rows_ok = (position[None, :] < work_len[:, None]).reshape(-1, 1)
    result = (
        jnp.where(rows_ok, output, 0.0)
        .astype(jnp.bfloat16)
        .reshape(block_count, block_len, model_width)
    )
    return (result, gated)


def shards(embed, lengths, w_in, w_out, cotangent):
    peer_count = lax.axis_size("peer")
    group_total = lax.axis_size("group")
    own_peer = lax.axis_index("peer")
    model_width = embed.shape[1]
    blocks = lengths.shape[1] // peer_count
    pair_depth = (blocks + peer_count - 1) // peer_count
    work_slots = cotangent.shape[0] // BLK
    block_lengths = lengths[0].reshape(peer_count, blocks)
    counts, prefix, block_rank, block_of, length_of = plan_tables(block_lengths)
    own_prefix = prefix[own_peer]
    own_count = counts[own_peer]
    dest_index = jnp.arange(peer_count, dtype=jnp.int32)
    pair_index = jnp.arange(pair_depth, dtype=jnp.int32)
    offset = ((dest_index - own_prefix) % peer_count)[:, None] + pair_index[None, :] * peer_count
    is_valid = offset < own_count
    picked = block_of[own_peer][jnp.minimum(offset, blocks - 1)]
    home_rows = embed.reshape(blocks, BLK, model_width)
    outgoing = jnp.where(is_valid[:, :, None, None], home_rows[picked], jnp.zeros((), embed.dtype))
    arrived = lax.all_to_all(
        outgoing.reshape(peer_count, pair_depth * BLK, model_width),
        "peer",
        split_axis=0,
        concat_axis=0,
        tiled=True,
    )
    arrived = arrived.reshape(peer_count, pair_depth, BLK, model_width)
    ticket = jnp.arange(work_slots, dtype=jnp.int32) * peer_count + own_peer
    source_end = prefix + counts
    source = jnp.sum((source_end[None, :] <= ticket[:, None]).astype(jnp.int32), axis=1)
    source = jnp.minimum(source, peer_count - 1)
    within = jnp.clip(ticket - prefix[source], 0, blocks - 1)
    work_len = length_of[source, within]
    work_rows = arrived[source, jnp.minimum(within // peer_count, pair_depth - 1)]
    result, pullback, gated = jax.vjp(
        lambda inputs: layer(inputs, work_len, w_in, w_out), work_rows, has_aux=True
    )
    cotan_blocks = cotangent.reshape(work_slots, BLK, model_width)
    (grad_work,) = pullback(cotan_blocks)
    back_offset = ((own_peer - prefix) % peer_count)[:, None] + pair_index[None, :] * peer_count
    back_valid = back_offset < counts[:, None]
    back_slot = jnp.clip((prefix[:, None] + back_offset) // peer_count, 0, work_slots - 1)
    returning = jnp.where(
        back_valid[:, :, None, None], grad_work[back_slot], jnp.zeros((), grad_work.dtype)
    )
    returned = lax.all_to_all(
        shortened(returning.reshape(peer_count, pair_depth * BLK, model_width)),
        "peer",
        split_axis=0,
        concat_axis=0,
        tiled=True,
    )
    returned = returned.reshape(peer_count, pair_depth, BLK, model_width)
    own_rank = block_rank[own_peer]
    target = (own_prefix + own_rank) % peer_count
    own_live = block_lengths[own_peer] > 0
    grad_back = jnp.where(
        own_live[:, None, None],
        returned[target, jnp.minimum(own_rank // peer_count, pair_depth - 1)],
        jnp.zeros((), returned.dtype),
    )
    attn_width = w_out.shape[0]
    grad_scale = 1.0 / math.sqrt(group_total * peer_count * work_slots * BLK)
    columns = lax.slice_in_dim(gated, 0, attn_width // peer_count * lax.axis_size("peer"), axis=1)
    grad_share = lax.psum_scatter(
        lax.dot_general(
            columns, cotangent, (((0,), (0,)), ((), ())), preferred_element_type=jnp.float32
        )
        * grad_scale,
        "peer",
        scatter_dimension=0,
        tiled=True,
    )
    grad_piece = lax.psum_scatter(grad_share, "group", scatter_dimension=1, tiled=True)
    return (result.reshape(-1, model_width), grad_back.reshape(-1, model_width), grad_piece)


MESH = pl.DeviceIdType.MESH
F32 = jnp.float32
BF16 = jnp.bfloat16
NT = (((1,), (1,)), ((), ()))
TN = (((0,), (0,)), ((), ()))


def toggled(index, bits):
    result = index
    bit = 1
    while bit <= bits:
        if bits & bit:
            result = result + bit * (1 - 2 * lax.rem(lax.div(index, bit), 2))
        bit *= 2
    return result


def dotf(a, b, dims=None):
    if dims is None:
        return jnp.dot(a, b, preferred_element_type=F32)
    return lax.dot_general(a, b, dims, preferred_element_type=F32)


def fused(
    peers,
    groups,
    len_ref,
    embed_hbm,
    w_in_hbm,
    w_out_hbm,
    cot_hbm,
    out_ref,
    grad_ref,
    gproj_ref,
    cot_v,
    embed_v,
    w_in_v,
    w_out_v,
    csend,
    crecv,
    osend,
    orecv,
    take_ref,
    pack_ref,
    x_ref,
    nrm_ref,
    inv_ref,
    act_ref,
    der_ref,
    wts_ref,
    dsw_ref,
    y_ref,
    gated_ref,
    inv2_ref,
    flag_ref,
    valid_ref,
    dg_ref,
    dproj_ref,
    dn_ref,
    gradp_ref,
    gfull_ref,
    core_send,
    core_recv,
    held_ref,
    z_send,
    z_recv,
    p_send,
    p_recv,
    in_sem,
    cs_sem,
    cr_sem,
    os_sem,
    or_sem,
    core_sem,
    zs_sem,
    zr_sem,
    ps_sem,
    pr_sem,
):
    me = lax.axis_index("peer")
    grp = lax.axis_index("group")
    rows, width = embed_v.shape
    work_rows = cot_v.shape[0]
    attn = w_out_v.shape[0]
    heads = attn // HD
    chunk = rows // peers
    blocks = rows // BLK
    total = len_ref.shape[1]
    tile = min(rows, 256)
    tiles = rows // tile
    per_tile = tile // chunk
    bit_count = peers.bit_length() - 1
    col = 256
    part = attn // peers
    gcols = width // groups
    half = peers // 2

    barrier = pltpu.get_barrier_semaphore()
    for j in range(1, peers):
        pl.semaphore_signal(
            barrier, inc=1, device_id={"peer": toggled(me, j)}, device_id_type=MESH
        )
    for d in range(1, groups):
        pl.semaphore_signal(
            barrier, inc=1, device_id={"group": lax.rem(grp + d, groups)}, device_id_type=MESH
        )

    loads = []
    for place, (src, dst) in enumerate(
        ((cot_hbm, cot_v), (embed_hbm, embed_v), (w_in_hbm, w_in_v), (w_out_hbm, w_out_v))
    ):
        load = pltpu.make_async_copy(src, dst, in_sem.at[place])
        load.start()
        loads.append(load)

    lens = len_ref[...]
    live = jnp.where(lens > 0, 1.0, 0.0).astype(F32)
    lane = lax.broadcasted_iota(jnp.int32, (1, total), 1)
    before = (
        lax.broadcasted_iota(jnp.int32, (total, total), 0)
        < lax.broadcasted_iota(jnp.int32, (total, total), 1)
    )
    before = jnp.where(before, 1.0, 0.0).astype(BF16)
    ticket = dotf(jnp.broadcast_to(live, (16, total)).astype(BF16), before).astype(jnp.int32)
    peer_end = (
        lax.broadcasted_iota(jnp.int32, (peers, total), 1)
        < (lax.broadcasted_iota(jnp.int32, (peers, total), 0) + 1) * blocks
    )
    ends = jnp.sum(jnp.where(peer_end, live, 0.0), axis=1, keepdims=True).astype(jnp.int32)
    own_prefix = jnp.sum(jnp.where(lane < me * blocks, live, 0.0), axis=1, keepdims=True).astype(
        jnp.int32
    )

    wlane = lax.broadcasted_iota(jnp.int32, (1, work_rows), 1)
    wticket = lax.shift_right_logical(wlane, 3) * peers + me
    passed = ends <= wticket
    source = jnp.sum(jnp.where(passed, 1, 0), axis=0, keepdims=True)
    start = jnp.max(jnp.where(passed, ends, 0), axis=0, keepdims=True)
    depth = lax.shift_right_logical(wticket - start, bit_count)
    wtarget = (source ^ me) * chunk + depth * BLK + (wlane & (BLK - 1))
    pack_ref[...] = jnp.where(
        lax.broadcasted_iota(jnp.int32, (rows, work_rows), 0) == wtarget, 1.0, 0.0
    ).astype(BF16)

    loads[0].wait()

    def pack(n, _):
        cols = pl.ds(pl.multiple_of(n * col, col), col)
        csend[:, cols] = dotf(pack_ref[...], cot_v[:, cols]).astype(BF16)
        return 0

    lax.fori_loop(0, width // col, pack, 0)
    pl.semaphore_wait(barrier, peers - 1 + groups - 1)

    def exchange(src, dst, s_sem, r_sem, j):
        span = pl.ds(j * chunk, chunk)
        return pltpu.make_async_remote_copy(
            src_ref=src.at[span],
            dst_ref=dst.at[span],
            send_sem=s_sem.at[j],
            recv_sem=r_sem.at[j],
            device_id={"peer": toggled(me, j)},
            device_id_type=MESH,
        )

    cot_moves = {j: exchange(csend, crecv, cs_sem, cr_sem, j) for j in range(1, peers)}
    for j in reversed(range(1, peers)):
        cot_moves[j].start()
    crecv[pl.ds(0, chunk), :] = csend[pl.ds(0, chunk), :]

    spot = lax.broadcasted_iota(jnp.int32, (16, total), 0)
    high = lax.shift_right_logical(ticket, 7)
    low = ticket & 127
    facts = jnp.where(spot == 0, high, jnp.where(spot == 1, low, lens)).astype(F32).astype(BF16)
    spread = (
        lax.broadcasted_iota(jnp.int32, (total, rows), 0)
        == me * blocks + lax.shift_right_logical(lax.broadcasted_iota(jnp.int32, (total, rows), 1), 3)
    )
    facts = dotf(facts, jnp.where(spread, 1.0, 0.0).astype(BF16)).astype(jnp.int32)
    hticket = facts[0:1] * 128 + facts[1:2]
    hlen = facts[2:3]
    hlane = lax.broadcasted_iota(jnp.int32, (1, rows), 1)
    rank = hticket - own_prefix
    target = (
        ((hticket & (peers - 1)) ^ me) * chunk
        + lax.shift_right_logical(rank, bit_count) * BLK
        + (hlane & (BLK - 1))
    )
    target = jnp.where(hlen > 0, target, -1)
    chosen = lax.broadcasted_iota(jnp.int32, (rows, rows), 0) == target
    take_ref[...] = jnp.where(chosen, 1.0, 0.0).astype(BF16)
    slot_len = jnp.sum(
        jnp.where(chosen, hlen.astype(F32), 0.0), axis=1, keepdims=True
    )
    row_in = lax.broadcasted_iota(jnp.int32, (rows, 1), 0) & (BLK - 1)
    valid_ref[...] = jnp.where(row_in.astype(F32) < slot_len, 1.0, 0.0)

    out_moves = {j: exchange(osend, orecv, os_sem, or_sem, j) for j in range(1, peers)}
    small = 32
    scale = HD ** (-0.5)
    sub = min(tile, 128)
    si = lax.broadcasted_iota(jnp.int32, (sub, sub), 0)
    sj = lax.broadcasted_iota(jnp.int32, (sub, sub), 1)
    near = (lax.shift_right_logical(si, 3) == lax.shift_right_logical(sj, 3)) & (sj <= si)
    near = jnp.where(near, 1.0, 0.0)

    loads[1].wait()
    for place, t in enumerate(reversed(range(tiles))):
        span = pl.ds(t * tile, tile)

        def pick(n, _):
            cols = pl.ds(pl.multiple_of(n * col, col), col)
            x_ref[span, cols] = dotf(take_ref[span, :], embed_v[:, cols]).astype(BF16)
            return 0

        lax.fori_loop(0, width // col, pick, 0)

        def norm(s, _):
            part_rows = pl.ds(pl.multiple_of(t * tile + s * small, small), small)
            x = x_ref[part_rows, :].astype(F32)
            x = x - jnp.mean(x, axis=1, keepdims=True)
            inv = lax.rsqrt(jnp.mean(x * x, axis=1, keepdims=True) + EPSILON)
            nrm_ref[part_rows, :] = (x * inv).astype(BF16)
            inv_ref[part_rows, :] = inv
            return 0

        lax.fori_loop(0, tile // small, norm, 0)
        if place == 0:
            loads[2].wait()

        def project(n, _):
            cols = pl.ds(pl.multiple_of(n * col, col), col)
            v = dotf(nrm_ref[span, :], w_in_v[:, cols])
            sig = 0.5 * jnp.tanh(0.5 * v) + 0.5
            act = v * sig
            act_ref[span, cols] = act.astype(BF16)
            der_ref[span, cols] = (sig + act * (1.0 - sig)).astype(BF16)
            return 0

        lax.fori_loop(0, 4 * attn // col, project, 0)

        def attend(s, _):
            sr = pl.ds(pl.multiple_of(t * tile + s * sub, sub), sub)
            allowed = near * valid_ref[sr, :]
            mixed = []
            for h in range(heads):
                hc = pl.ds(h * HD, HD)
                values = act_ref[sr, pl.ds(attn + h * HD, HD)]
                queries = act_ref[sr, pl.ds(2 * attn + h * HD, HD)]
                keys = act_ref[sr, pl.ds(3 * attn + h * HD, HD)]
                score = dotf(queries, keys, NT) * scale
                sig = 0.5 * jnp.tanh(0.5 * score) + 0.5
                weight = score * sig
                slope = (sig + weight * (1.0 - sig)) * scale
                weight = jnp.where(allowed > 0.0, weight, 0.0).astype(BF16)
                wts_ref[sr, pl.ds(h * sub, sub)] = weight
                dsw_ref[sr, pl.ds(h * sub, sub)] = jnp.where(allowed > 0.0, slope, 0.0).astype(BF16)
                mixed.append(dotf(weight, values))
            mixed = jnp.concatenate(mixed, axis=1)
            mixed = mixed - jnp.mean(mixed, axis=1, keepdims=True)
            var = jnp.mean(mixed * mixed, axis=1, keepdims=True)
            inv = lax.rsqrt(jnp.maximum(var, MIX_FLOOR))
            y = mixed * inv
            inv2_ref[sr, :] = inv
            flag_ref[sr, :] = jnp.where(
                var > MIX_FLOOR, 1.0, jnp.where(var == MIX_FLOOR, 0.5, 0.0)
            )
            y_ref[sr, :] = y.astype(BF16)
            gated_ref[sr, :] = (y * act_ref[sr, pl.ds(0, attn)].astype(F32)).astype(BF16)
            return 0

        lax.fori_loop(0, tile // sub, attend, 0)
        if place == 0:
            loads[3].wait()

        def produce(n, _):
            cols = pl.ds(pl.multiple_of(n * col, col), col)
            out = x_ref[span, cols].astype(F32) + dotf(gated_ref[span, :], w_out_v[:, cols])
            osend[span, cols] = jnp.where(valid_ref[span, :] > 0.0, out, 0.0).astype(BF16)
            return 0

        lax.fori_loop(0, width // col, produce, 0)
        for j in reversed(range(t * per_tile, (t + 1) * per_tile)):
            if j:
                out_moves[j].start()
    orecv[pl.ds(0, chunk), :] = osend[pl.ds(0, chunk), :]

    for j in range(1, peers):
        cot_moves[j].wait_recv()

    def mask(s, _):
        sr = pl.ds(pl.multiple_of(s * small, small), small)
        got = crecv[sr, :].astype(F32)
        crecv[sr, :] = jnp.where(valid_ref[sr, :] > 0.0, got, 0.0).astype(BF16)
        return 0

    lax.fori_loop(0, rows // small, mask, 0)

    def outer(n, _):
        cols = pl.ds(pl.multiple_of(n * col, col), col)
        gfull_ref[:, cols] = dotf(gated_ref[...], crecv[:, cols], TN)
        return 0

    lax.fori_loop(0, width // col, outer, 0)
    for m in range(half):
        theirs = pl.multiple_of(toggled(me, 2 * m + 1) * part, part)
        core_send[pl.ds(m * part, part), :] = gfull_ref[pl.ds(theirs, part), :].astype(BF16)
    core_move = pltpu.make_async_remote_copy(
        src_ref=core_send,
        dst_ref=core_recv,
        send_sem=core_sem.at[0],
        recv_sem=core_sem.at[1],
        device_id={"peer": toggled(me, 1)},
        device_id_type=MESH,
    )
    core_move.start()

    def backward(t):
        span = pl.ds(t * tile, tile)

        def back_out(n, _):
            cols = pl.ds(pl.multiple_of(n * col, col), col)
            dg_ref[:, cols] = dotf(crecv[span, :], w_out_v[cols, :], NT).astype(BF16)
            return 0

        lax.fori_loop(0, attn // col, back_out, 0)

        def back_attend(s, _):
            here = pl.ds(pl.multiple_of(s * sub, sub), sub)
            sr = pl.ds(pl.multiple_of(t * tile + s * sub, sub), sub)
            dg = dg_ref[here, :].astype(F32)
            y = y_ref[sr, :].astype(F32)
            gate = pl.ds(0, attn)
            dgate = (dg * y).astype(BF16).astype(F32)
            dproj_ref[here, gate] = (dgate * der_ref[sr, gate].astype(F32)).astype(BF16)
            dy = dg * act_ref[sr, gate].astype(F32)
            slant = jnp.mean(dy * y, axis=1, keepdims=True) * flag_ref[sr, :]
            dc = (dy - y * slant) * inv2_ref[sr, :]
            dmix = (dc - jnp.mean(dc, axis=1, keepdims=True)).astype(BF16)
            for h in range(heads):
                vc = pl.ds(attn + h * HD, HD)
                qc = pl.ds(2 * attn + h * HD, HD)
                kc = pl.ds(3 * attn + h * HD, HD)
                dm = dmix[:, h * HD : (h + 1) * HD]
                dw = dotf(dm, act_ref[sr, vc], NT).astype(BF16).astype(F32)
                ds = (dw * dsw_ref[sr, pl.ds(h * sub, sub)].astype(F32)).astype(BF16)
                dv = dotf(wts_ref[sr, pl.ds(h * sub, sub)], dm, TN)
                dq = dotf(ds, act_ref[sr, kc])
                dk = dotf(ds, act_ref[sr, qc], TN)
                for place_of, grad in ((vc, dv), (qc, dq), (kc, dk)):
                    grad = grad.astype(BF16).astype(F32)
                    dproj_ref[here, place_of] = (grad * der_ref[sr, place_of].astype(F32)).astype(BF16)
            return 0

        lax.fori_loop(0, tile // sub, back_attend, 0)

        def back_in(n, _):
            cols = pl.ds(pl.multiple_of(n * col, col), col)
            dn_ref[:, cols] = dotf(dproj_ref[...], w_in_v[cols, :], NT).astype(BF16)
            return 0

        lax.fori_loop(0, width // col, back_in, 0)

        def back_norm(s, _):
            here = pl.ds(pl.multiple_of(s * small, small), small)
            sr = pl.ds(pl.multiple_of(t * tile + s * small, small), small)
            dn = dn_ref[here, :].astype(F32)
            xh = nrm_ref[sr, :].astype(F32)
            dc = (dn - xh * jnp.mean(dn * xh, axis=1, keepdims=True)) * inv_ref[sr, :]
            dx = dc - jnp.mean(dc, axis=1, keepdims=True)
            gradp_ref[sr, :] = (crecv[sr, :].astype(F32) + dx).astype(BF16)
            return 0

        lax.fori_loop(0, tile // small, back_norm, 0)

    z_moves = [
        pltpu.make_async_remote_copy(
            src_ref=z_send.at[d - 1],
            dst_ref=z_recv.at[d - 1],
            send_sem=zs_sem.at[d - 1],
            recv_sem=zr_sem.at[d - 1],
            device_id={"group": lax.rem(grp + d, groups)},
            device_id_type=MESH,
        )
        for d in range(1, groups)
    ]
    p_moves = [
        pltpu.make_async_remote_copy(
            src_ref=p_send.at[m - 1],
            dst_ref=p_recv.at[m - 1],
            send_sem=ps_sem.at[m - 1],
            recv_sem=pr_sem.at[m - 1],
            device_id={"peer": toggled(me, 2 * m)},
            device_id_type=MESH,
        )
        for m in range(1, half)
    ]
    for t in range(tiles):
        backward(t)
        if t == 0:
            core_move.wait_recv()
            for d in range(groups):
                theirs = pl.ds(pl.multiple_of(lax.rem(grp + d, groups) * gcols, gcols), gcols)
                for m in range(half):
                    ours = pl.multiple_of(toggled(me, 2 * m) * part, part)
                    mr = pl.ds(m * part, part)
                    pair = gfull_ref[pl.ds(ours, part), theirs] + core_recv[mr, theirs].astype(F32)
                    if d:
                        z_send[d - 1, mr, :] = pair.astype(BF16)
                    else:
                        held_ref[mr, :] = pair
                if d:
                    z_moves[d - 1].start()

    for move in z_moves:
        move.wait_recv()
    for m in reversed(range(half)):
        mr = pl.ds(m * part, part)
        share = held_ref[mr, :]
        for d in range(1, groups):
            share = share + z_recv[d - 1, mr, :].astype(F32)
        if m:
            p_send[m - 1] = share.astype(BF16)
            p_moves[m - 1].start()
        else:
            held_ref[mr, :] = share

    def unpack_grad(n, _):
        cols = pl.ds(pl.multiple_of(n * col, col), col)
        grad_ref[:, cols] = dotf(take_ref[...], gradp_ref[:, cols], TN).astype(BF16)
        return 0

    lax.fori_loop(0, width // col, unpack_grad, 0)

    for j in range(1, peers):
        out_moves[j].wait_recv()

    def unpack_out(n, _):
        cols = pl.ds(pl.multiple_of(n * col, col), col)
        out_ref[:, cols] = dotf(pack_ref[...], orecv[:, cols], TN).astype(BF16)
        return 0

    lax.fori_loop(0, width // col, unpack_out, 0)

    share = held_ref[pl.ds(0, part), :]
    for m in range(1, half):
        p_moves[m - 1].wait_recv()
        share = share + p_recv[m - 1].astype(F32)
    gproj_ref[...] = share * (1.0 / math.sqrt(groups * peers * work_rows))

    for j in range(1, peers):
        cot_moves[j].wait_send()
        out_moves[j].wait_send()
    core_move.wait_send()
    for move in z_moves + p_moves:
        move.wait_send()


def fused_shards(embed, lengths, w_in, w_out, cotangent):
    peers = lax.axis_size("peer")
    groups = lax.axis_size("group")
    rows, width = embed.shape
    work_rows = cotangent.shape[0]
    attn = w_out.shape[0]
    tile = min(rows, 256)
    sub = min(tile, 128)
    heads = attn // HD
    part = attn // peers
    gcols = width // groups
    half = peers // 2
    vmem = pltpu.VMEM
    dma = pltpu.SemaphoreType.DMA
    scratch = [
        vmem((work_rows, width), BF16),
        vmem((rows, width), BF16),
        vmem(w_in.shape, BF16),
        vmem(w_out.shape, BF16),
        vmem((rows, width), BF16),
        vmem((rows, width), BF16),
        vmem((rows, width), BF16),
        vmem((rows, width), BF16),
        vmem((rows, rows), BF16),
        vmem((rows, work_rows), BF16),
        vmem((rows, width), BF16),
        vmem((rows, width), BF16),
        vmem((rows, 1), F32),
        vmem((rows, 4 * attn), BF16),
        vmem((rows, 4 * attn), BF16),
        vmem((rows, heads * sub), BF16),
        vmem((rows, heads * sub), BF16),
        vmem((rows, attn), BF16),
        vmem((rows, attn), BF16),
        vmem((rows, 1), F32),
        vmem((rows, 1), F32),
        vmem((rows, 1), F32),
        vmem((tile, attn), BF16),
        vmem((tile, 4 * attn), BF16),
        vmem((tile, width), BF16),
        vmem((rows, width), BF16),
        vmem((attn, width), F32),
        vmem((half * part, width), BF16),
        vmem((half * part, width), BF16),
        vmem((half * part, gcols), F32),
        vmem((groups - 1, half * part, gcols), BF16),
        vmem((groups - 1, half * part, gcols), BF16),
        vmem((half - 1, part, gcols), BF16),
        vmem((half - 1, part, gcols), BF16),
        dma((4,)),
        dma((peers,)),
        dma((peers,)),
        dma((peers,)),
        dma((peers,)),
        dma((2,)),
        dma((groups - 1,)),
        dma((groups - 1,)),
        dma((half - 1,)),
        dma((half - 1,)),
    ]
    anywhere = pl.BlockSpec(memory_space=pl.ANY)
    resident = pl.BlockSpec(memory_space=pltpu.VMEM)
    return pl.pallas_call(
        functools.partial(fused, peers, groups),
        out_shape=(
            jax.ShapeDtypeStruct((work_rows, width), BF16),
            jax.ShapeDtypeStruct((rows, width), BF16),
            jax.ShapeDtypeStruct((part, gcols), F32),
        ),
        in_specs=[resident] + [anywhere] * 4,
        out_specs=(resident, resident, resident),
        scratch_shapes=scratch,
        compiler_params=pltpu.CompilerParams(
            collective_id=0, has_side_effects=True, vmem_limit_bytes=48 * 1024 * 1024
        ),
        cost_estimate=pl.CostEstimate(
            flops=2 * rows * width * attn * 11,
            bytes_accessed=2 * (w_in.size + w_out.size + 3 * rows * width),
            transcendentals=rows * attn * 5,
        ),
    )(lengths, embed, w_in, w_out, cotangent)


def fits(mesh):
    peers = mesh.shape["peer"]

    def check(embed, lengths, w_out):
        rows = embed.shape[0] // (peers * mesh.shape["group"])
        part, left = divmod(w_out.shape[0], peers)
        return (
            peers & (peers - 1) == 0
            and peers >= 4
            and mesh.shape["group"] > 1
            and rows % (16 * peers) == 0
            and rows % 256 == 0
            and 256 % (rows // peers) == 0
            and left == 0
            and part % 16 == 0
            and embed.shape[1] % (256 * mesh.shape["group"]) == 0
            and lengths.shape[1] * BLK == rows * peers
        )

    return check


def solution(mesh):
    placed = (P(("group", "peer"), None), P("group", None), P(), P(), P(("group", "peer"), None))

    def mapped(body):
        return jax.shard_map(
            body,
            mesh=mesh,
            in_specs=placed,
            out_specs=(P(("group", "peer"), None), P(("group", "peer"), None), P("peer", "group")),
            check_vma=False,
        )

    def run(embed, lengths, w_in, w_out, cotangent):
        body = fused_shards if fits(mesh)(embed, lengths, w_out) else shards
        return mapped(body)(embed, lengths, w_in, w_out, cotangent)

    return run
```

```python
import functools
import math

import jax
import jax.numpy as jnp
from jax import lax
from jax.experimental import pallas as pl
from jax.experimental.pallas import tpu as pltpu
from jax.sharding import PartitionSpec as P

HD = 128
BLK = 8


EPSILON = 1e-06
MIX_FLOOR = 1.0


def shortened(shard):

    def short(part):
        return part.astype(jnp.bfloat16) if part.dtype == jnp.float32 else part

    return jax.tree.map(short, shard)


def plan_tables(block_lengths):
    block_total = block_lengths.shape[1]
    is_live = (block_lengths > 0).astype(jnp.int32)
    counts = jnp.sum(is_live, axis=1)
    prefix = jnp.cumsum(counts) - counts
    block_rank = jnp.cumsum(is_live, axis=1) - is_live
    slot_index = jnp.arange(block_total, dtype=jnp.int32)
    chosen = (block_rank[:, :, None] == slot_index[None, None, :]) & (is_live[:, :, None] > 0)
    chosen_int = chosen.astype(jnp.int32)
    block_of = jnp.sum(chosen_int * slot_index[None, :, None], axis=1)
    length_of = jnp.sum(chosen_int * block_lengths[:, :, None], axis=1)
    return (counts, prefix, block_rank, block_of, length_of)


def layer(inputs, work_len, w_in, w_out):
    block_count = inputs.shape[0]
    block_len = inputs.shape[1]
    model_width = inputs.shape[2]
    attn_width = w_out.shape[0]
    head_count = attn_width // HD
    floated = inputs.astype(jnp.float32)
    row_mean = jnp.mean(floated, axis=-1, keepdims=True)
    centred = floated - row_mean
    row_var = jnp.mean(centred * centred, axis=-1, keepdims=True)
    normed = (centred * lax.rsqrt(row_var + EPSILON)).astype(jnp.bfloat16)
    projected = jnp.dot(normed.reshape(-1, model_width), w_in, preferred_element_type=jnp.float32)
    activated = jax.nn.silu(projected).astype(jnp.bfloat16)
    gating = activated[:, :attn_width]
    values = activated[:, attn_width : 2 * attn_width].reshape(
        block_count, block_len, head_count, HD
    )
    queries = activated[:, 2 * attn_width : 3 * attn_width].reshape(
        block_count, block_len, head_count, HD
    )
    key_rows = activated[:, 3 * attn_width :].reshape(block_count, block_len, head_count, HD)
    scores = jnp.einsum(
        "bihd,bjhd->bhij", queries.astype(jnp.float32), key_rows.astype(jnp.float32)
    ) * HD ** (-0.5)
    position = jnp.arange(block_len, dtype=jnp.int32)
    causal = position[None, :] <= position[:, None]
    limit = work_len[:, None, None, None]
    allowed = (
        causal[None, None, :, :]
        & (position[None, None, None, :] < limit)
        & (position[None, None, :, None] < limit)
    )
    weights = jnp.where(allowed, jax.nn.silu(scores), 0.0).astype(jnp.bfloat16)
    mixed = jnp.einsum("bhij,bjhd->bihd", weights.astype(jnp.float32), values.astype(jnp.float32))
    mixed = mixed.reshape(block_count * block_len, attn_width)
    mix_mean = jnp.mean(mixed, axis=-1, keepdims=True)
    mix_centred = mixed - mix_mean
    mix_var = jnp.mean(mix_centred * mix_centred, axis=-1, keepdims=True)
    gated = (
        mix_centred * lax.rsqrt(jnp.maximum(mix_var, MIX_FLOOR)) * gating.astype(jnp.float32)
    ).astype(jnp.bfloat16)
    output = floated.reshape(-1, model_width) + jnp.dot(
        gated, w_out, preferred_element_type=jnp.float32
    )
    rows_ok = (position[None, :] < work_len[:, None]).reshape(-1, 1)
    result = (
        jnp.where(rows_ok, output, 0.0)
        .astype(jnp.bfloat16)
        .reshape(block_count, block_len, model_width)
    )
    return (result, gated)


def shards(embed, lengths, w_in, w_out, cotangent):
    peer_count = lax.axis_size("peer")
    group_total = lax.axis_size("group")
    own_peer = lax.axis_index("peer")
    model_width = embed.shape[1]
    blocks = lengths.shape[1] // peer_count
    pair_depth = (blocks + peer_count - 1) // peer_count
    work_slots = cotangent.shape[0] // BLK
    block_lengths = lengths[0].reshape(peer_count, blocks)
    counts, prefix, block_rank, block_of, length_of = plan_tables(block_lengths)
    own_prefix = prefix[own_peer]
    own_count = counts[own_peer]
    dest_index = jnp.arange(peer_count, dtype=jnp.int32)
    pair_index = jnp.arange(pair_depth, dtype=jnp.int32)
    offset = ((dest_index - own_prefix) % peer_count)[:, None] + pair_index[None, :] * peer_count
    is_valid = offset < own_count
    picked = block_of[own_peer][jnp.minimum(offset, blocks - 1)]
    home_rows = embed.reshape(blocks, BLK, model_width)
    outgoing = jnp.where(is_valid[:, :, None, None], home_rows[picked], jnp.zeros((), embed.dtype))
    arrived = lax.all_to_all(
        outgoing.reshape(peer_count, pair_depth * BLK, model_width),
        "peer",
        split_axis=0,
        concat_axis=0,
        tiled=True,
    )
    arrived = arrived.reshape(peer_count, pair_depth, BLK, model_width)
    ticket = jnp.arange(work_slots, dtype=jnp.int32) * peer_count + own_peer
    source_end = prefix + counts
    source = jnp.sum((source_end[None, :] <= ticket[:, None]).astype(jnp.int32), axis=1)
    source = jnp.minimum(source, peer_count - 1)
    within = jnp.clip(ticket - prefix[source], 0, blocks - 1)
    work_len = length_of[source, within]
    work_rows = arrived[source, jnp.minimum(within // peer_count, pair_depth - 1)]
    result, pullback, gated = jax.vjp(
        lambda inputs: layer(inputs, work_len, w_in, w_out), work_rows, has_aux=True
    )
    cotan_blocks = cotangent.reshape(work_slots, BLK, model_width)
    (grad_work,) = pullback(cotan_blocks)
    back_offset = ((own_peer - prefix) % peer_count)[:, None] + pair_index[None, :] * peer_count
    back_valid = back_offset < counts[:, None]
    back_slot = jnp.clip((prefix[:, None] + back_offset) // peer_count, 0, work_slots - 1)
    returning = jnp.where(
        back_valid[:, :, None, None], grad_work[back_slot], jnp.zeros((), grad_work.dtype)
    )
    returned = lax.all_to_all(
        shortened(returning.reshape(peer_count, pair_depth * BLK, model_width)),
        "peer",
        split_axis=0,
        concat_axis=0,
        tiled=True,
    )
    returned = returned.reshape(peer_count, pair_depth, BLK, model_width)
    own_rank = block_rank[own_peer]
    target = (own_prefix + own_rank) % peer_count
    own_live = block_lengths[own_peer] > 0
    grad_back = jnp.where(
        own_live[:, None, None],
        returned[target, jnp.minimum(own_rank // peer_count, pair_depth - 1)],
        jnp.zeros((), returned.dtype),
    )
    attn_width = w_out.shape[0]
    grad_scale = 1.0 / math.sqrt(group_total * peer_count * work_slots * BLK)
    columns = lax.slice_in_dim(gated, 0, attn_width // peer_count * lax.axis_size("peer"), axis=1)
    grad_share = lax.psum_scatter(
        lax.dot_general(
            columns, cotangent, (((0,), (0,)), ((), ())), preferred_element_type=jnp.float32
        )
        * grad_scale,
        "peer",
        scatter_dimension=0,
        tiled=True,
    )
    grad_piece = lax.psum_scatter(grad_share, "group", scatter_dimension=1, tiled=True)
    return (result.reshape(-1, model_width), grad_back.reshape(-1, model_width), grad_piece)


MESH = pl.DeviceIdType.MESH
F32 = jnp.float32
BF16 = jnp.bfloat16
NT = (((1,), (1,)), ((), ()))
TN = (((0,), (0,)), ((), ()))


def toggled(index, bits):
    result = index
    bit = 1
    while bit <= bits:
        if bits & bit:
            result = result + bit * (1 - 2 * lax.rem(lax.div(index, bit), 2))
        bit *= 2
    return result


def dotf(a, b, dims=None):
    if dims is None:
        return jnp.dot(a, b, preferred_element_type=F32)
    return lax.dot_general(a, b, dims, preferred_element_type=F32)


def fused(
    peers,
    groups,
    len_hbm,
    embed_hbm,
    w_in_hbm,
    w_out_hbm,
    cot_hbm,
    out_ref,
    grad_ref,
    gproj_ref,
    len_ref,
    cot_v,
    embed_v,
    w_in_v,
    w_out_v,
    csend,
    crecv,
    osend,
    orecv,
    take_ref,
    pack_ref,
    unpack_ref,
    untake_ref,
    gated_t_ref,
    x_ref,
    nrm_ref,
    inv_ref,
    act_ref,
    der_ref,
    wts_ref,
    dsw_ref,
    y_ref,
    gated_ref,
    inv2_ref,
    flag_ref,
    valid_ref,
    dg_ref,
    dproj_ref,
    dn_ref,
    gradp_ref,
    gfull_ref,
    core_send,
    core_recv,
    held_ref,
    z_send,
    z_recv,
    p_send,
    p_recv,
    in_sem,
    cs_sem,
    cr_sem,
    os_sem,
    or_sem,
    core_sem,
    zs_sem,
    zr_sem,
    ps_sem,
    pr_sem,
):
    me = lax.axis_index("peer")
    grp = lax.axis_index("group")
    rows, width = embed_v.shape
    work_rows = cot_v.shape[0]
    attn = w_out_v.shape[0]
    heads = attn // HD
    chunk = rows // peers
    blocks = rows // BLK
    total = len_ref.shape[1]
    tile = rows
    tiles = rows // tile
    per_tile = tile // chunk
    bit_count = peers.bit_length() - 1
    col = 256
    part = attn // peers
    gcols = width // groups
    half = peers // 2

    len_load = pltpu.make_async_copy(len_hbm, len_ref, in_sem.at[4])
    len_load.start()
    loads = []
    for place, (src, dst) in enumerate(
        (
            (cot_hbm, cot_v),
            (embed_hbm, embed_v),
            (w_in_hbm, w_in_v),
            (w_out_hbm, w_out_v),
        )
    ):
        load = pltpu.make_async_copy(src, dst, in_sem.at[place])
        load.start()
        loads.append(load)

    barrier = pltpu.get_barrier_semaphore()
    for j in range(1, peers):
        pl.semaphore_signal(
            barrier, inc=1, device_id={"peer": toggled(me, j)}, device_id_type=MESH
        )
    for d in range(1, groups):
        pl.semaphore_signal(
            barrier, inc=1, device_id={"group": lax.rem(grp + d, groups)}, device_id_type=MESH
        )

    len_load.wait()
    lens = len_ref[...]
    live = jnp.where(lens > 0, 1.0, 0.0).astype(F32)
    lane = lax.broadcasted_iota(jnp.int32, (1, total), 1)
    before = (
        lax.broadcasted_iota(jnp.int32, (total, total), 0)
        < lax.broadcasted_iota(jnp.int32, (total, total), 1)
    )
    before = jnp.where(before, 1.0, 0.0).astype(BF16)
    ticket = dotf(jnp.broadcast_to(live, (16, total)).astype(BF16), before).astype(jnp.int32)
    peer_end = (
        lax.broadcasted_iota(jnp.int32, (peers, total), 1)
        < (lax.broadcasted_iota(jnp.int32, (peers, total), 0) + 1) * blocks
    )
    ends = jnp.sum(jnp.where(peer_end, live, 0.0), axis=1, keepdims=True).astype(jnp.int32)
    own_prefix = jnp.sum(jnp.where(lane < me * blocks, live, 0.0), axis=1, keepdims=True).astype(
        jnp.int32
    )

    wlane = lax.broadcasted_iota(jnp.int32, (1, work_rows), 1)
    wticket = lax.shift_right_logical(wlane, 3) * peers + me
    passed = ends <= wticket
    source = jnp.sum(jnp.where(passed, 1, 0), axis=0, keepdims=True)
    start = jnp.max(jnp.where(passed, ends, 0), axis=0, keepdims=True)
    depth = lax.shift_right_logical(wticket - start, bit_count)
    wtarget = (source ^ me) * chunk + depth * BLK + (wlane & (BLK - 1))
    pack_ref[...] = jnp.where(
        lax.broadcasted_iota(jnp.int32, (rows, work_rows), 0) == wtarget, 1.0, 0.0
    ).astype(BF16)

    loads[0].wait()

    def pack(n, _):
        cols = pl.ds(pl.multiple_of(n * col, col), col)
        csend[:, cols] = dotf(pack_ref[...], cot_v[:, cols]).astype(BF16)
        return 0

    lax.fori_loop(0, width // col, pack, 0, unroll=True)
    pl.semaphore_wait(barrier, peers - 1 + groups - 1)

    def exchange(src, dst, s_sem, r_sem, j):
        span = pl.ds(j * chunk, chunk)
        return pltpu.make_async_remote_copy(
            src_ref=src.at[span],
            dst_ref=dst.at[span],
            send_sem=s_sem.at[j],
            recv_sem=r_sem.at[j],
            device_id={"peer": toggled(me, j)},
            device_id_type=MESH,
        )

    cot_moves = {j: exchange(csend, crecv, cs_sem, cr_sem, j) for j in range(1, peers)}
    for j in reversed(range(1, peers)):
        cot_moves[j].start()
    crecv[pl.ds(0, chunk), :] = csend[pl.ds(0, chunk), :]

    spot = lax.broadcasted_iota(jnp.int32, (16, total), 0)
    high = lax.shift_right_logical(ticket, 7)
    low = ticket & 127
    facts = jnp.where(spot == 0, high, jnp.where(spot == 1, low, lens)).astype(F32).astype(BF16)
    spread = (
        lax.broadcasted_iota(jnp.int32, (total, rows), 0)
        == me * blocks + lax.shift_right_logical(lax.broadcasted_iota(jnp.int32, (total, rows), 1), 3)
    )
    facts = dotf(facts, jnp.where(spread, 1.0, 0.0).astype(BF16)).astype(jnp.int32)
    hticket = facts[0:1] * 128 + facts[1:2]
    hlen = facts[2:3]
    hlane = lax.broadcasted_iota(jnp.int32, (1, rows), 1)
    rank = hticket - own_prefix
    target = (
        ((hticket & (peers - 1)) ^ me) * chunk
        + lax.shift_right_logical(rank, bit_count) * BLK
        + (hlane & (BLK - 1))
    )
    target = jnp.where(hlen > 0, target, -1)
    chosen = lax.broadcasted_iota(jnp.int32, (rows, rows), 0) == target
    take_ref[...] = jnp.where(chosen, 1.0, 0.0).astype(BF16)
    slot_len = jnp.sum(
        jnp.where(chosen, hlen.astype(F32), 0.0), axis=1, keepdims=True
    )
    row_in = lax.broadcasted_iota(jnp.int32, (rows, 1), 0) & (BLK - 1)
    valid_ref[...] = jnp.where(row_in.astype(F32) < slot_len, 1.0, 0.0)

    def upright(line):
        return jnp.transpose(jnp.broadcast_to(line.astype(F32), (128, line.shape[1])))[:, 0:1]

    slots = lax.broadcasted_iota(jnp.int32, (1, rows), 1).astype(F32)
    untake_ref[...] = jnp.where(upright(target) == slots, 1.0, 0.0).astype(BF16)
    unpack_ref[...] = jnp.where(upright(wtarget) == slots, 1.0, 0.0).astype(BF16)

    out_moves = {j: exchange(osend, orecv, os_sem, or_sem, j) for j in range(1, peers)}
    small = 64
    scale = HD ** (-0.5)
    sub = min(tile, 128)
    si = lax.broadcasted_iota(jnp.int32, (sub, sub), 0)
    sj = lax.broadcasted_iota(jnp.int32, (sub, sub), 1)
    near = (lax.shift_right_logical(si, 3) == lax.shift_right_logical(sj, 3)) & (sj <= si)
    near = jnp.where(near, 1.0, 0.0)

    loads[1].wait()
    for place, t in enumerate(reversed(range(tiles))):
        span = pl.ds(t * tile, tile)

        def pick(n, _):
            cols = pl.ds(pl.multiple_of(n * col, col), col)
            x_ref[span, cols] = dotf(take_ref[span, :], embed_v[:, cols]).astype(BF16)
            return 0

        lax.fori_loop(0, width // col, pick, 0, unroll=True)

        def norm(s, _):
            part_rows = pl.ds(pl.multiple_of(t * tile + s * small, small), small)
            x = x_ref[part_rows, :].astype(F32)
            x = x - jnp.mean(x, axis=1, keepdims=True)
            inv = lax.rsqrt(jnp.mean(x * x, axis=1, keepdims=True) + EPSILON)
            nrm_ref[part_rows, :] = (x * inv).astype(BF16)
            inv_ref[part_rows, :] = inv
            return 0

        lax.fori_loop(0, tile // small, norm, 0, unroll=4)
        if place == 0:
            loads[2].wait()

        def project(n, _):
            cols = pl.ds(pl.multiple_of(n * col, col), col)
            v = dotf(nrm_ref[span, :], w_in_v[:, cols])
            sig = 0.5 * jnp.tanh(0.5 * v) + 0.5
            act = v * sig
            act_ref[span, cols] = act.astype(BF16)
            der_ref[span, cols] = (sig + act * (1.0 - sig)).astype(BF16)
            return 0

        lax.fori_loop(0, 4 * attn // col, project, 0, unroll=4)

        def attend(s, _):
            sr = pl.ds(pl.multiple_of(t * tile + s * sub, sub), sub)
            allowed = near * valid_ref[sr, :]
            mixed = []
            for h in range(heads):
                hc = pl.ds(h * HD, HD)
                values = act_ref[sr, pl.ds(attn + h * HD, HD)]
                queries = act_ref[sr, pl.ds(2 * attn + h * HD, HD)]
                keys = act_ref[sr, pl.ds(3 * attn + h * HD, HD)]
                score = dotf(queries, keys, NT) * scale
                sig = 0.5 * jnp.tanh(0.5 * score) + 0.5
                weight = score * sig
                slope = (sig + weight * (1.0 - sig)) * scale
                weight = jnp.where(allowed > 0.0, weight, 0.0).astype(BF16)
                wts_ref[sr, pl.ds(h * sub, sub)] = weight
                dsw_ref[sr, pl.ds(h * sub, sub)] = jnp.where(allowed > 0.0, slope, 0.0).astype(BF16)
                mixed.append(dotf(weight, values))
            mixed = jnp.concatenate(mixed, axis=1)
            mixed = mixed - jnp.mean(mixed, axis=1, keepdims=True)
            var = jnp.mean(mixed * mixed, axis=1, keepdims=True)
            inv = lax.rsqrt(jnp.maximum(var, MIX_FLOOR))
            y = mixed * inv
            inv2_ref[sr, :] = inv
            flag_ref[sr, :] = jnp.where(
                var > MIX_FLOOR, 1.0, jnp.where(var == MIX_FLOOR, 0.5, 0.0)
            )
            y_ref[sr, :] = y.astype(BF16)
            gated = y * act_ref[sr, pl.ds(0, attn)].astype(F32)
            gated_ref[sr, :] = gated.astype(BF16)
            gated_t_ref[:, sr] = jnp.transpose(gated).astype(BF16)
            return 0

        lax.fori_loop(0, tile // sub, attend, 0, unroll=2)
        if place == 0:
            loads[3].wait()

        def produce(n, _):
            cols = pl.ds(pl.multiple_of(n * col, col), col)
            out = x_ref[span, cols].astype(F32) + dotf(gated_ref[span, :], w_out_v[:, cols])
            osend[span, cols] = jnp.where(valid_ref[span, :] > 0.0, out, 0.0).astype(BF16)
            return 0

        lax.fori_loop(0, width // col, produce, 0, unroll=True)
        for j in reversed(range(t * per_tile, (t + 1) * per_tile)):
            if j:
                out_moves[j].start()
    orecv[pl.ds(0, chunk), :] = osend[pl.ds(0, chunk), :]

    for j in range(1, peers):
        cot_moves[j].wait_recv()

    def mask(s, _):
        sr = pl.ds(pl.multiple_of(s * small, small), small)
        got = crecv[sr, :].astype(F32)
        crecv[sr, :] = jnp.where(valid_ref[sr, :] > 0.0, got, 0.0).astype(BF16)
        return 0

    lax.fori_loop(0, rows // small, mask, 0, unroll=True)

    def outer(n, _):
        cols = pl.ds(pl.multiple_of(n * col, col), col)
        gfull_ref[:, cols] = dotf(gated_t_ref[...], crecv[:, cols])
        return 0

    lax.fori_loop(0, width // col, outer, 0, unroll=True)
    for m in range(half):
        theirs = pl.multiple_of(toggled(me, 2 * m + 1) * part, part)
        core_send[pl.ds(m * part, part), :] = gfull_ref[pl.ds(theirs, part), :].astype(BF16)
    core_move = pltpu.make_async_remote_copy(
        src_ref=core_send,
        dst_ref=core_recv,
        send_sem=core_sem.at[0],
        recv_sem=core_sem.at[1],
        device_id={"peer": toggled(me, 1)},
        device_id_type=MESH,
    )
    core_move.start()

    def back_out(n, _):
        cols = pl.ds(pl.multiple_of(n * col, col), col)
        dg_ref[:, cols] = dotf(crecv[...], w_out_v[cols, :], NT).astype(BF16)
        return 0

    lax.fori_loop(0, attn // col, back_out, 0, unroll=True)

    def backward(t):
        def back_attend(s, _):
            here = pl.ds(pl.multiple_of(s * sub, sub), sub)
            sr = pl.ds(pl.multiple_of(t * tile + s * sub, sub), sub)
            dg = dg_ref[here, :].astype(F32)
            y = y_ref[sr, :].astype(F32)
            gate = pl.ds(0, attn)
            dgate = (dg * y).astype(BF16).astype(F32)
            dproj_ref[here, gate] = (dgate * der_ref[sr, gate].astype(F32)).astype(BF16)
            dy = dg * act_ref[sr, gate].astype(F32)
            slant = jnp.mean(dy * y, axis=1, keepdims=True) * flag_ref[sr, :]
            dc = (dy - y * slant) * inv2_ref[sr, :]
            dmix = (dc - jnp.mean(dc, axis=1, keepdims=True)).astype(BF16)
            for h in range(heads):
                vc = pl.ds(attn + h * HD, HD)
                qc = pl.ds(2 * attn + h * HD, HD)
                kc = pl.ds(3 * attn + h * HD, HD)
                dm = dmix[:, h * HD : (h + 1) * HD]
                dw = dotf(dm, act_ref[sr, vc], NT).astype(BF16).astype(F32)
                ds = (dw * dsw_ref[sr, pl.ds(h * sub, sub)].astype(F32)).astype(BF16)
                dv = dotf(wts_ref[sr, pl.ds(h * sub, sub)], dm, TN)
                dq = dotf(ds, act_ref[sr, kc])
                dk = dotf(ds, act_ref[sr, qc], TN)
                for place_of, grad in ((vc, dv), (qc, dq), (kc, dk)):
                    grad = grad.astype(BF16).astype(F32)
                    dproj_ref[here, place_of] = (grad * der_ref[sr, place_of].astype(F32)).astype(BF16)
            return 0

        lax.fori_loop(0, tile // sub, back_attend, 0, unroll=2)

        def back_in(n, _):
            cols = pl.ds(pl.multiple_of(n * col, col), col)
            dn_ref[:, cols] = dotf(dproj_ref[...], w_in_v[cols, :], NT).astype(BF16)
            return 0

        lax.fori_loop(0, width // col, back_in, 0, unroll=True)

        def back_norm(s, _):
            here = pl.ds(pl.multiple_of(s * small, small), small)
            sr = pl.ds(pl.multiple_of(t * tile + s * small, small), small)
            dn = dn_ref[here, :].astype(F32)
            xh = nrm_ref[sr, :].astype(F32)
            dc = (dn - xh * jnp.mean(dn * xh, axis=1, keepdims=True)) * inv_ref[sr, :]
            dx = dc - jnp.mean(dc, axis=1, keepdims=True)
            gradp_ref[sr, :] = (crecv[sr, :].astype(F32) + dx).astype(BF16)
            return 0

        lax.fori_loop(0, tile // small, back_norm, 0, unroll=4)

    z_moves = [
        pltpu.make_async_remote_copy(
            src_ref=z_send.at[d - 1],
            dst_ref=z_recv.at[d - 1],
            send_sem=zs_sem.at[d - 1],
            recv_sem=zr_sem.at[d - 1],
            device_id={"group": lax.rem(grp + d, groups)},
            device_id_type=MESH,
        )
        for d in range(1, groups)
    ]
    p_moves = [
        pltpu.make_async_remote_copy(
            src_ref=p_send.at[m - 1],
            dst_ref=p_recv.at[m - 1],
            send_sem=ps_sem.at[m - 1],
            recv_sem=pr_sem.at[m - 1],
            device_id={"peer": toggled(me, 2 * m)},
            device_id_type=MESH,
        )
        for m in range(1, half)
    ]
    core_move.wait_recv()
    for d in reversed(range(groups)):
        theirs = pl.ds(pl.multiple_of(lax.rem(grp + d, groups) * gcols, gcols), gcols)
        for m in range(half):
            ours = pl.multiple_of(toggled(me, 2 * m) * part, part)
            mr = pl.ds(m * part, part)
            pair = gfull_ref[pl.ds(ours, part), theirs] + core_recv[mr, theirs].astype(F32)
            if d:
                z_send[d - 1, mr, :] = pair.astype(BF16)
            else:
                held_ref[mr, :] = pair
        if d:
            z_moves[d - 1].start()
    backward(0)

    for move in z_moves:
        move.wait_recv()
    for m in reversed(range(half)):
        mr = pl.ds(m * part, part)
        share = held_ref[mr, :]
        for d in range(1, groups):
            share = share + z_recv[d - 1, mr, :].astype(F32)
        if m:
            p_send[m - 1] = share.astype(BF16)
            p_moves[m - 1].start()
        else:
            held_ref[mr, :] = share

    def unpack_grad(n, _):
        cols = pl.ds(pl.multiple_of(n * col, col), col)
        grad_ref[:, cols] = dotf(untake_ref[...], gradp_ref[:, cols]).astype(BF16)
        return 0

    lax.fori_loop(0, width // col, unpack_grad, 0, unroll=True)

    for j in range(1, peers):
        out_moves[j].wait_recv()

    def unpack_out(n, _):
        cols = pl.ds(pl.multiple_of(n * col, col), col)
        out_ref[:, cols] = dotf(unpack_ref[...], orecv[:, cols]).astype(BF16)
        return 0

    lax.fori_loop(0, width // col, unpack_out, 0, unroll=True)

    share = held_ref[pl.ds(0, part), :]
    for m in range(1, half):
        p_moves[m - 1].wait_recv()
        share = share + p_recv[m - 1].astype(F32)
    gproj_ref[...] = share * (1.0 / math.sqrt(groups * peers * work_rows))

    for j in range(1, peers):
        cot_moves[j].wait_send()
        out_moves[j].wait_send()
    core_move.wait_send()
    for move in z_moves + p_moves:
        move.wait_send()


def fused_shards(embed, lengths, w_in, w_out, cotangent):
    peers = lax.axis_size("peer")
    groups = lax.axis_size("group")
    rows, width = embed.shape
    work_rows = cotangent.shape[0]
    attn = w_out.shape[0]
    tile = rows
    sub = min(tile, 128)
    heads = attn // HD
    part = attn // peers
    gcols = width // groups
    half = peers // 2
    vmem = pltpu.VMEM
    dma = pltpu.SemaphoreType.DMA
    scratch = [
        vmem(lengths.shape, jnp.int32),
        vmem((work_rows, width), BF16),
        vmem((rows, width), BF16),
        vmem(w_in.shape, BF16),
        vmem(w_out.shape, BF16),
        vmem((rows, width), BF16),
        vmem((rows, width), BF16),
        vmem((rows, width), BF16),
        vmem((rows, width), BF16),
        vmem((rows, rows), BF16),
        vmem((rows, work_rows), BF16),
        vmem((work_rows, rows), BF16),
        vmem((rows, rows), BF16),
        vmem((attn, rows), BF16),
        vmem((rows, width), BF16),
        vmem((rows, width), BF16),
        vmem((rows, 1), F32),
        vmem((rows, 4 * attn), BF16),
        vmem((rows, 4 * attn), BF16),
        vmem((rows, heads * sub), BF16),
        vmem((rows, heads * sub), BF16),
        vmem((rows, attn), BF16),
        vmem((rows, attn), BF16),
        vmem((rows, 1), F32),
        vmem((rows, 1), F32),
        vmem((rows, 1), F32),
        vmem((tile, attn), BF16),
        vmem((tile, 4 * attn), BF16),
        vmem((tile, width), BF16),
        vmem((rows, width), BF16),
        vmem((attn, width), F32),
        vmem((half * part, width), BF16),
        vmem((half * part, width), BF16),
        vmem((half * part, gcols), F32),
        vmem((groups - 1, half * part, gcols), BF16),
        vmem((groups - 1, half * part, gcols), BF16),
        vmem((half - 1, part, gcols), BF16),
        vmem((half - 1, part, gcols), BF16),
        dma((5,)),
        dma((peers,)),
        dma((peers,)),
        dma((peers,)),
        dma((peers,)),
        dma((2,)),
        dma((groups - 1,)),
        dma((groups - 1,)),
        dma((half - 1,)),
        dma((half - 1,)),
    ]
    pinned = pl.BlockSpec(memory_space=pltpu.HBM)
    resident = pl.BlockSpec(memory_space=pltpu.VMEM)
    return pl.pallas_call(
        functools.partial(fused, peers, groups),
        out_shape=(
            jax.ShapeDtypeStruct((work_rows, width), BF16),
            jax.ShapeDtypeStruct((rows, width), BF16),
            jax.ShapeDtypeStruct((part, gcols), F32),
        ),
        in_specs=[pinned] * 5,
        out_specs=(resident, resident, resident),
        scratch_shapes=scratch,
        compiler_params=pltpu.CompilerParams(
            collective_id=0, has_side_effects=True, vmem_limit_bytes=60 * 1024 * 1024
        ),
        cost_estimate=pl.CostEstimate(
            flops=2 * rows * width * attn * 11,
            bytes_accessed=2 * (w_in.size + w_out.size + 3 * rows * width),
            transcendentals=rows * attn * 5,
        ),
    )(lengths, embed, w_in, w_out, cotangent)


def fits(mesh):
    peers = mesh.shape["peer"]

    def check(embed, lengths, w_out):
        rows = embed.shape[0] // (peers * mesh.shape["group"])
        part, left = divmod(w_out.shape[0], peers)
        return (
            peers & (peers - 1) == 0
            and peers >= 4
            and mesh.shape["group"] > 1
            and rows % (16 * peers) == 0
            and rows % 256 == 0
            and 256 % (rows // peers) == 0
            and left == 0
            and part % 16 == 0
            and embed.shape[1] % (256 * mesh.shape["group"]) == 0
            and lengths.shape[1] * BLK == rows * peers
        )

    return check


def solution(mesh):
    placed = (P(("group", "peer"), None), P("group", None), P(), P(), P(("group", "peer"), None))

    def mapped(body):
        return jax.shard_map(
            body,
            mesh=mesh,
            in_specs=placed,
            out_specs=(P(("group", "peer"), None), P(("group", "peer"), None), P("peer", "group")),
            check_vma=False,
        )

    def run(embed, lengths, w_in, w_out, cotangent):
        body = fused_shards if fits(mesh)(embed, lengths, w_out) else shards
        return mapped(body)(embed, lengths, w_in, w_out, cotangent)

    return run
```

```python
import functools
import math

import jax
import jax.numpy as jnp
from jax import lax
from jax.experimental import pallas as pl
from jax.experimental.pallas import tpu as pltpu
from jax.sharding import PartitionSpec as P

HD = 128
BLK = 8


EPSILON = 1e-06
MIX_FLOOR = 1.0


def shortened(shard):

    def short(part):
        return part.astype(jnp.bfloat16) if part.dtype == jnp.float32 else part

    return jax.tree.map(short, shard)


def plan_tables(block_lengths):
    block_total = block_lengths.shape[1]
    is_live = (block_lengths > 0).astype(jnp.int32)
    counts = jnp.sum(is_live, axis=1)
    prefix = jnp.cumsum(counts) - counts
    block_rank = jnp.cumsum(is_live, axis=1) - is_live
    slot_index = jnp.arange(block_total, dtype=jnp.int32)
    chosen = (block_rank[:, :, None] == slot_index[None, None, :]) & (is_live[:, :, None] > 0)
    chosen_int = chosen.astype(jnp.int32)
    block_of = jnp.sum(chosen_int * slot_index[None, :, None], axis=1)
    length_of = jnp.sum(chosen_int * block_lengths[:, :, None], axis=1)
    return (counts, prefix, block_rank, block_of, length_of)


def layer(inputs, work_len, w_in, w_out):
    block_count = inputs.shape[0]
    block_len = inputs.shape[1]
    model_width = inputs.shape[2]
    attn_width = w_out.shape[0]
    head_count = attn_width // HD
    floated = inputs.astype(jnp.float32)
    row_mean = jnp.mean(floated, axis=-1, keepdims=True)
    centred = floated - row_mean
    row_var = jnp.mean(centred * centred, axis=-1, keepdims=True)
    normed = (centred * lax.rsqrt(row_var + EPSILON)).astype(jnp.bfloat16)
    projected = jnp.dot(normed.reshape(-1, model_width), w_in, preferred_element_type=jnp.float32)
    activated = jax.nn.silu(projected).astype(jnp.bfloat16)
    gating = activated[:, :attn_width]
    values = activated[:, attn_width : 2 * attn_width].reshape(
        block_count, block_len, head_count, HD
    )
    queries = activated[:, 2 * attn_width : 3 * attn_width].reshape(
        block_count, block_len, head_count, HD
    )
    key_rows = activated[:, 3 * attn_width :].reshape(block_count, block_len, head_count, HD)
    scores = jnp.einsum(
        "bihd,bjhd->bhij", queries.astype(jnp.float32), key_rows.astype(jnp.float32)
    ) * HD ** (-0.5)
    position = jnp.arange(block_len, dtype=jnp.int32)
    causal = position[None, :] <= position[:, None]
    limit = work_len[:, None, None, None]
    allowed = (
        causal[None, None, :, :]
        & (position[None, None, None, :] < limit)
        & (position[None, None, :, None] < limit)
    )
    weights = jnp.where(allowed, jax.nn.silu(scores), 0.0).astype(jnp.bfloat16)
    mixed = jnp.einsum("bhij,bjhd->bihd", weights.astype(jnp.float32), values.astype(jnp.float32))
    mixed = mixed.reshape(block_count * block_len, attn_width)
    mix_mean = jnp.mean(mixed, axis=-1, keepdims=True)
    mix_centred = mixed - mix_mean
    mix_var = jnp.mean(mix_centred * mix_centred, axis=-1, keepdims=True)
    gated = (
        mix_centred * lax.rsqrt(jnp.maximum(mix_var, MIX_FLOOR)) * gating.astype(jnp.float32)
    ).astype(jnp.bfloat16)
    output = floated.reshape(-1, model_width) + jnp.dot(
        gated, w_out, preferred_element_type=jnp.float32
    )
    rows_ok = (position[None, :] < work_len[:, None]).reshape(-1, 1)
    result = (
        jnp.where(rows_ok, output, 0.0)
        .astype(jnp.bfloat16)
        .reshape(block_count, block_len, model_width)
    )
    return (result, gated)


def shards(embed, lengths, w_in, w_out, cotangent):
    peer_count = lax.axis_size("peer")
    group_total = lax.axis_size("group")
    own_peer = lax.axis_index("peer")
    model_width = embed.shape[1]
    blocks = lengths.shape[1] // peer_count
    pair_depth = (blocks + peer_count - 1) // peer_count
    work_slots = cotangent.shape[0] // BLK
    block_lengths = lengths[0].reshape(peer_count, blocks)
    counts, prefix, block_rank, block_of, length_of = plan_tables(block_lengths)
    own_prefix = prefix[own_peer]
    own_count = counts[own_peer]
    dest_index = jnp.arange(peer_count, dtype=jnp.int32)
    pair_index = jnp.arange(pair_depth, dtype=jnp.int32)
    offset = ((dest_index - own_prefix) % peer_count)[:, None] + pair_index[None, :] * peer_count
    is_valid = offset < own_count
    picked = block_of[own_peer][jnp.minimum(offset, blocks - 1)]
    home_rows = embed.reshape(blocks, BLK, model_width)
    outgoing = jnp.where(is_valid[:, :, None, None], home_rows[picked], jnp.zeros((), embed.dtype))
    arrived = lax.all_to_all(
        outgoing.reshape(peer_count, pair_depth * BLK, model_width),
        "peer",
        split_axis=0,
        concat_axis=0,
        tiled=True,
    )
    arrived = arrived.reshape(peer_count, pair_depth, BLK, model_width)
    ticket = jnp.arange(work_slots, dtype=jnp.int32) * peer_count + own_peer
    source_end = prefix + counts
    source = jnp.sum((source_end[None, :] <= ticket[:, None]).astype(jnp.int32), axis=1)
    source = jnp.minimum(source, peer_count - 1)
    within = jnp.clip(ticket - prefix[source], 0, blocks - 1)
    work_len = length_of[source, within]
    work_rows = arrived[source, jnp.minimum(within // peer_count, pair_depth - 1)]
    result, pullback, gated = jax.vjp(
        lambda inputs: layer(inputs, work_len, w_in, w_out), work_rows, has_aux=True
    )
    cotan_blocks = cotangent.reshape(work_slots, BLK, model_width)
    (grad_work,) = pullback(cotan_blocks)
    back_offset = ((own_peer - prefix) % peer_count)[:, None] + pair_index[None, :] * peer_count
    back_valid = back_offset < counts[:, None]
    back_slot = jnp.clip((prefix[:, None] + back_offset) // peer_count, 0, work_slots - 1)
    returning = jnp.where(
        back_valid[:, :, None, None], grad_work[back_slot], jnp.zeros((), grad_work.dtype)
    )
    returned = lax.all_to_all(
        shortened(returning.reshape(peer_count, pair_depth * BLK, model_width)),
        "peer",
        split_axis=0,
        concat_axis=0,
        tiled=True,
    )
    returned = returned.reshape(peer_count, pair_depth, BLK, model_width)
    own_rank = block_rank[own_peer]
    target = (own_prefix + own_rank) % peer_count
    own_live = block_lengths[own_peer] > 0
    grad_back = jnp.where(
        own_live[:, None, None],
        returned[target, jnp.minimum(own_rank // peer_count, pair_depth - 1)],
        jnp.zeros((), returned.dtype),
    )
    attn_width = w_out.shape[0]
    grad_scale = 1.0 / math.sqrt(group_total * peer_count * work_slots * BLK)
    columns = lax.slice_in_dim(gated, 0, attn_width // peer_count * lax.axis_size("peer"), axis=1)
    grad_share = lax.psum_scatter(
        lax.dot_general(
            columns, cotangent, (((0,), (0,)), ((), ())), preferred_element_type=jnp.float32
        )
        * grad_scale,
        "peer",
        scatter_dimension=0,
        tiled=True,
    )
    grad_piece = lax.psum_scatter(grad_share, "group", scatter_dimension=1, tiled=True)
    return (result.reshape(-1, model_width), grad_back.reshape(-1, model_width), grad_piece)


MESH = pl.DeviceIdType.MESH
F32 = jnp.float32
BF16 = jnp.bfloat16
NT = (((1,), (1,)), ((), ()))
TN = (((0,), (0,)), ((), ()))


def toggled(index, bits):
    result = index
    bit = 1
    while bit <= bits:
        if bits & bit:
            result = result + bit * (1 - 2 * lax.rem(lax.div(index, bit), 2))
        bit *= 2
    return result


def dotf(a, b, dims=None):
    if dims is None:
        return jnp.dot(a, b, preferred_element_type=F32)
    return lax.dot_general(a, b, dims, preferred_element_type=F32)


def fused(
    peers,
    groups,
    len_hbm,
    embed_hbm,
    w_in_hbm,
    w_out_hbm,
    cot_hbm,
    out_ref,
    grad_ref,
    gproj_ref,
    len_ref,
    cot_v,
    embed_v,
    w_in_v,
    w_out_v,
    csend,
    crecv,
    osend,
    orecv,
    take_ref,
    pack_ref,
    unpack_ref,
    untake_ref,
    gated_t_ref,
    x_ref,
    nrm_ref,
    inv_ref,
    act_ref,
    der_ref,
    wts_ref,
    dsw_ref,
    y_ref,
    gated_ref,
    inv2_ref,
    flag_ref,
    valid_ref,
    dg_ref,
    dproj_ref,
    dn_ref,
    gradp_ref,
    gfull_ref,
    core_send,
    core_recv,
    held_ref,
    kept_ref,
    z_send,
    z_recv,
    p_send,
    p_recv,
    q_send,
    q_recv,
    r_send,
    r_recv,
    in_sem,
    cs_sem,
    cr_sem,
    os_sem,
    or_sem,
    core_sem,
    zs_sem,
    zr_sem,
    ps_sem,
    pr_sem,
    qs_sem,
    qr_sem,
    rs_sem,
    rr_sem,
):
    me = lax.axis_index("peer")
    grp = lax.axis_index("group")
    rows, width = embed_v.shape
    work_rows = cot_v.shape[0]
    attn = w_out_v.shape[0]
    heads = attn // HD
    chunk = rows // peers
    blocks = rows // BLK
    total = len_ref.shape[1]
    tile = rows
    tiles = rows // tile
    bit_count = peers.bit_length() - 1
    col = 256
    part = attn // peers
    gcols = width // groups
    half = peers // 2
    zpart = part // 2
    qpart = part - zpart

    len_load = pltpu.make_async_copy(len_hbm, len_ref, in_sem.at[4])
    len_load.start()
    loads = []
    for place, (src, dst) in enumerate(
        (
            (cot_hbm, cot_v),
            (embed_hbm, embed_v),
            (w_in_hbm, w_in_v),
            (w_out_hbm, w_out_v),
        )
    ):
        load = pltpu.make_async_copy(src, dst, in_sem.at[place])
        load.start()
        loads.append(load)

    barrier = pltpu.get_barrier_semaphore()
    for j in range(1, peers):
        pl.semaphore_signal(
            barrier, inc=1, device_id={"peer": toggled(me, j)}, device_id_type=MESH
        )
    for d in range(1, groups):
        pl.semaphore_signal(
            barrier, inc=1, device_id={"group": lax.rem(grp + d, groups)}, device_id_type=MESH
        )

    len_load.wait()
    lens = len_ref[...]
    live = jnp.where(lens > 0, 1.0, 0.0).astype(F32)
    lane = lax.broadcasted_iota(jnp.int32, (1, total), 1)
    before = (
        lax.broadcasted_iota(jnp.int32, (total, total), 0)
        < lax.broadcasted_iota(jnp.int32, (total, total), 1)
    )
    before = jnp.where(before, 1.0, 0.0).astype(BF16)
    ticket = dotf(jnp.broadcast_to(live, (16, total)).astype(BF16), before).astype(jnp.int32)
    peer_end = (
        lax.broadcasted_iota(jnp.int32, (peers, total), 1)
        < (lax.broadcasted_iota(jnp.int32, (peers, total), 0) + 1) * blocks
    )
    ends = jnp.sum(jnp.where(peer_end, live, 0.0), axis=1, keepdims=True).astype(jnp.int32)
    own_prefix = jnp.sum(jnp.where(lane < me * blocks, live, 0.0), axis=1, keepdims=True).astype(
        jnp.int32
    )

    wlane = lax.broadcasted_iota(jnp.int32, (1, work_rows), 1)
    wticket = lax.shift_right_logical(wlane, 3) * peers + me
    passed = ends <= wticket
    source = jnp.sum(jnp.where(passed, 1, 0), axis=0, keepdims=True)
    start = jnp.max(jnp.where(passed, ends, 0), axis=0, keepdims=True)
    depth = lax.shift_right_logical(wticket - start, bit_count)
    wtarget = (source ^ me) * chunk + depth * BLK + (wlane & (BLK - 1))
    pack_ref[...] = jnp.where(
        lax.broadcasted_iota(jnp.int32, (rows, work_rows), 0) == wtarget, 1.0, 0.0
    ).astype(BF16)

    loads[0].wait()

    def exchange(src, dst, s_sem, r_sem, j):
        span = pl.ds(j * chunk, chunk)
        return pltpu.make_async_remote_copy(
            src_ref=src.at[span],
            dst_ref=dst.at[span],
            send_sem=s_sem.at[j],
            recv_sem=r_sem.at[j],
            device_id={"peer": toggled(me, j)},
            device_id_type=MESH,
        )

    cot_moves = {j: exchange(csend, crecv, cs_sem, cr_sem, j) for j in range(1, peers)}
    for u in reversed(range(half)):
        duo = pl.ds(u * 2 * chunk, 2 * chunk)
        csend[duo, :] = dotf(pack_ref[duo, :], cot_v[...]).astype(BF16)
        if u == half - 1:
            pl.semaphore_wait(barrier, peers - 1 + groups - 1)
        for j in (2 * u + 1, 2 * u):
            if j:
                cot_moves[j].start()
    crecv[pl.ds(0, chunk), :] = csend[pl.ds(0, chunk), :]

    spot = lax.broadcasted_iota(jnp.int32, (16, total), 0)
    high = lax.shift_right_logical(ticket, 7)
    low = ticket & 127
    facts = jnp.where(spot == 0, high, jnp.where(spot == 1, low, lens)).astype(F32).astype(BF16)
    spread = (
        lax.broadcasted_iota(jnp.int32, (total, rows), 0)
        == me * blocks + lax.shift_right_logical(lax.broadcasted_iota(jnp.int32, (total, rows), 1), 3)
    )
    facts = dotf(facts, jnp.where(spread, 1.0, 0.0).astype(BF16)).astype(jnp.int32)
    hticket = facts[0:1] * 128 + facts[1:2]
    hlen = facts[2:3]
    hlane = lax.broadcasted_iota(jnp.int32, (1, rows), 1)
    rank = hticket - own_prefix
    target = (
        ((hticket & (peers - 1)) ^ me) * chunk
        + lax.shift_right_logical(rank, bit_count) * BLK
        + (hlane & (BLK - 1))
    )
    target = jnp.where(hlen > 0, target, -1)
    chosen = lax.broadcasted_iota(jnp.int32, (rows, rows), 0) == target
    take_ref[...] = jnp.where(chosen, 1.0, 0.0).astype(BF16)
    slot_len = jnp.sum(
        jnp.where(chosen, hlen.astype(F32), 0.0), axis=1, keepdims=True
    )
    row_in = lax.broadcasted_iota(jnp.int32, (rows, 1), 0) & (BLK - 1)
    valid_ref[...] = jnp.where(row_in.astype(F32) < slot_len, 1.0, 0.0)

    def upright(line):
        return jnp.transpose(jnp.broadcast_to(line.astype(F32), (128, line.shape[1])))[:, 0:1]

    slots = lax.broadcasted_iota(jnp.int32, (1, rows), 1).astype(F32)
    untake_ref[...] = jnp.where(upright(target) == slots, 1.0, 0.0).astype(BF16)
    unpack_ref[...] = jnp.where(upright(wtarget) == slots, 1.0, 0.0).astype(BF16)

    out_moves = {j: exchange(osend, orecv, os_sem, or_sem, j) for j in range(1, peers)}
    small = 64
    scale = HD ** (-0.5)
    sub = min(tile, 128)
    si = lax.broadcasted_iota(jnp.int32, (sub, sub), 0)
    sj = lax.broadcasted_iota(jnp.int32, (sub, sub), 1)
    near = (lax.shift_right_logical(si, 3) == lax.shift_right_logical(sj, 3)) & (sj <= si)
    near = jnp.where(near, 1.0, 0.0)

    loads[1].wait()
    for place, t in enumerate(reversed(range(tiles))):
        span = pl.ds(t * tile, tile)

        def pick(n, _):
            cols = pl.ds(pl.multiple_of(n * col, col), col)
            x_ref[span, cols] = dotf(take_ref[span, :], embed_v[:, cols]).astype(BF16)
            return 0

        lax.fori_loop(0, width // col, pick, 0, unroll=True)

        def norm(s, _):
            part_rows = pl.ds(pl.multiple_of(t * tile + s * small, small), small)
            x = x_ref[part_rows, :].astype(F32)
            x = x - jnp.mean(x, axis=1, keepdims=True)
            inv = lax.rsqrt(jnp.mean(x * x, axis=1, keepdims=True) + EPSILON)
            nrm_ref[part_rows, :] = (x * inv).astype(BF16)
            inv_ref[part_rows, :] = inv
            return 0

        lax.fori_loop(0, tile // small, norm, 0, unroll=4)
        if place == 0:
            loads[2].wait()

        def project(n, _):
            cols = pl.ds(pl.multiple_of(n * col, col), col)
            v = dotf(nrm_ref[span, :], w_in_v[:, cols])
            sig = 0.5 * jnp.tanh(0.5 * v) + 0.5
            act = v * sig
            act_ref[span, cols] = act.astype(BF16)
            der_ref[span, cols] = (sig + act * (1.0 - sig)).astype(BF16)
            return 0

        lax.fori_loop(0, 4 * attn // col, project, 0, unroll=4)

        def attend(s, _):
            sr = pl.ds(pl.multiple_of(t * tile + s * sub, sub), sub)
            allowed = near * valid_ref[sr, :]
            mixed = []
            for h in range(heads):
                hc = pl.ds(h * HD, HD)
                values = act_ref[sr, pl.ds(attn + h * HD, HD)]
                queries = act_ref[sr, pl.ds(2 * attn + h * HD, HD)]
                keys = act_ref[sr, pl.ds(3 * attn + h * HD, HD)]
                score = dotf(queries, keys, NT) * scale
                sig = 0.5 * jnp.tanh(0.5 * score) + 0.5
                weight = score * sig
                slope = (sig + weight * (1.0 - sig)) * scale
                weight = jnp.where(allowed > 0.0, weight, 0.0).astype(BF16)
                wts_ref[sr, pl.ds(h * sub, sub)] = weight
                dsw_ref[sr, pl.ds(h * sub, sub)] = jnp.where(allowed > 0.0, slope, 0.0).astype(BF16)
                mixed.append(dotf(weight, values))
            mixed = jnp.concatenate(mixed, axis=1)
            mixed = mixed - jnp.mean(mixed, axis=1, keepdims=True)
            var = jnp.mean(mixed * mixed, axis=1, keepdims=True)
            inv = lax.rsqrt(jnp.maximum(var, MIX_FLOOR))
            y = mixed * inv
            inv2_ref[sr, :] = inv
            flag_ref[sr, :] = jnp.where(
                var > MIX_FLOOR, 1.0, jnp.where(var == MIX_FLOOR, 0.5, 0.0)
            )
            y_ref[sr, :] = y.astype(BF16)
            gated = y * act_ref[sr, pl.ds(0, attn)].astype(F32)
            gated_ref[sr, :] = gated.astype(BF16)
            gated_t_ref[:, sr] = jnp.transpose(gated).astype(BF16)
            return 0

        lax.fori_loop(0, tile // sub, attend, 0, unroll=2)
        if place == 0:
            loads[3].wait()

        def produce(n, _):
            cols = pl.ds(pl.multiple_of(n * col, col), col)
            out = x_ref[span, cols].astype(F32) + dotf(gated_ref[span, :], w_out_v[:, cols])
            osend[span, cols] = jnp.where(valid_ref[span, :] > 0.0, out, 0.0).astype(BF16)
            return 0

        lax.fori_loop(0, width // col, produce, 0, unroll=True)
    orecv[pl.ds(0, chunk), :] = osend[pl.ds(0, chunk), :]

    for j in range(1, peers):
        cot_moves[j].wait_recv()
    for j in reversed(range(1, peers)):
        out_moves[j].start()

    def mask(s, _):
        sr = pl.ds(pl.multiple_of(s * small, small), small)
        got = crecv[sr, :].astype(F32)
        crecv[sr, :] = jnp.where(valid_ref[sr, :] > 0.0, got, 0.0).astype(BF16)
        return 0

    lax.fori_loop(0, rows // small, mask, 0, unroll=True)

    def outer(n, _):
        cols = pl.ds(pl.multiple_of(n * col, col), col)
        gfull_ref[:, cols] = dotf(gated_t_ref[...], crecv[:, cols])
        return 0

    lax.fori_loop(0, width // col, outer, 0, unroll=True)
    for m in range(half):
        theirs = pl.multiple_of(toggled(me, 2 * m + 1) * part, part)
        core_send[pl.ds(m * part, part), :] = gfull_ref[pl.ds(theirs, part), :].astype(BF16)
    core_move = pltpu.make_async_remote_copy(
        src_ref=core_send,
        dst_ref=core_recv,
        send_sem=core_sem.at[0],
        recv_sem=core_sem.at[1],
        device_id={"peer": toggled(me, 1)},
        device_id_type=MESH,
    )
    core_move.start()

    def back_out(n, _):
        cols = pl.ds(pl.multiple_of(n * col, col), col)
        dg_ref[:, cols] = dotf(crecv[...], w_out_v[cols, :], NT).astype(BF16)
        return 0

    lax.fori_loop(0, attn // col, back_out, 0, unroll=True)

    def backward(t):
        def back_attend(s, _):
            here = pl.ds(pl.multiple_of(s * sub, sub), sub)
            sr = pl.ds(pl.multiple_of(t * tile + s * sub, sub), sub)
            dg = dg_ref[here, :].astype(F32)
            y = y_ref[sr, :].astype(F32)
            gate = pl.ds(0, attn)
            dgate = (dg * y).astype(BF16).astype(F32)
            dproj_ref[here, gate] = (dgate * der_ref[sr, gate].astype(F32)).astype(BF16)
            dy = dg * act_ref[sr, gate].astype(F32)
            slant = jnp.mean(dy * y, axis=1, keepdims=True) * flag_ref[sr, :]
            dc = (dy - y * slant) * inv2_ref[sr, :]
            dmix = (dc - jnp.mean(dc, axis=1, keepdims=True)).astype(BF16)
            for h in range(heads):
                vc = pl.ds(attn + h * HD, HD)
                qc = pl.ds(2 * attn + h * HD, HD)
                kc = pl.ds(3 * attn + h * HD, HD)
                dm = dmix[:, h * HD : (h + 1) * HD]
                dw = dotf(dm, act_ref[sr, vc], NT).astype(BF16).astype(F32)
                ds = (dw * dsw_ref[sr, pl.ds(h * sub, sub)].astype(F32)).astype(BF16)
                dv = dotf(wts_ref[sr, pl.ds(h * sub, sub)], dm, TN)
                dq = dotf(ds, act_ref[sr, kc])
                dk = dotf(ds, act_ref[sr, qc], TN)
                for place_of, grad in ((vc, dv), (qc, dq), (kc, dk)):
                    grad = grad.astype(BF16).astype(F32)
                    dproj_ref[here, place_of] = (grad * der_ref[sr, place_of].astype(F32)).astype(BF16)
            return 0

        lax.fori_loop(0, tile // sub, back_attend, 0, unroll=2)

        def back_in(n, _):
            cols = pl.ds(pl.multiple_of(n * col, col), col)
            dn_ref[:, cols] = dotf(dproj_ref[...], w_in_v[cols, :], NT).astype(BF16)
            return 0

        lax.fori_loop(0, width // col, back_in, 0, unroll=True)

        for move in q_moves:
            move.wait_recv()
        mine = pl.ds(pl.multiple_of(grp * gcols, gcols), gcols)
        for d in reversed(range(groups)):
            theirs = pl.ds(pl.multiple_of(lax.rem(grp + d, groups) * gcols, gcols), gcols)
            share = kept_ref[:, theirs]
            for m in range(1, half):
                share = share + q_recv[m - 1, :, theirs].astype(F32)
            if d:
                r_send[d - 1] = share.astype(BF16)
                r_moves[d - 1].start()
            else:
                kept_ref[:, mine] = share

        for move in z_moves:
            move.wait_recv()
        for m in reversed(range(half)):
            mr = pl.ds(m * zpart, zpart)
            share = held_ref[mr, :]
            for d in range(1, groups):
                share = share + z_recv[d - 1, mr, :].astype(F32)
            if m:
                p_send[m - 1] = share.astype(BF16)
                p_moves[m - 1].start()
            else:
                held_ref[mr, :] = share

        def back_norm(s, _):
            here = pl.ds(pl.multiple_of(s * small, small), small)
            sr = pl.ds(pl.multiple_of(t * tile + s * small, small), small)
            dn = dn_ref[here, :].astype(F32)
            xh = nrm_ref[sr, :].astype(F32)
            dc = (dn - xh * jnp.mean(dn * xh, axis=1, keepdims=True)) * inv_ref[sr, :]
            dx = dc - jnp.mean(dc, axis=1, keepdims=True)
            gradp_ref[sr, :] = (crecv[sr, :].astype(F32) + dx).astype(BF16)
            return 0

        lax.fori_loop(0, tile // small, back_norm, 0, unroll=4)

    z_moves = [
        pltpu.make_async_remote_copy(
            src_ref=z_send.at[d - 1],
            dst_ref=z_recv.at[d - 1],
            send_sem=zs_sem.at[d - 1],
            recv_sem=zr_sem.at[d - 1],
            device_id={"group": lax.rem(grp + d, groups)},
            device_id_type=MESH,
        )
        for d in range(1, groups)
    ]
    r_moves = [
        pltpu.make_async_remote_copy(
            src_ref=r_send.at[d - 1],
            dst_ref=r_recv.at[d - 1],
            send_sem=rs_sem.at[d - 1],
            recv_sem=rr_sem.at[d - 1],
            device_id={"group": lax.rem(grp + d, groups)},
            device_id_type=MESH,
        )
        for d in range(1, groups)
    ]
    q_moves = [
        pltpu.make_async_remote_copy(
            src_ref=q_send.at[m - 1],
            dst_ref=q_recv.at[m - 1],
            send_sem=qs_sem.at[m - 1],
            recv_sem=qr_sem.at[m - 1],
            device_id={"peer": toggled(me, 2 * m)},
            device_id_type=MESH,
        )
        for m in range(1, half)
    ]
    p_moves = [
        pltpu.make_async_remote_copy(
            src_ref=p_send.at[m - 1],
            dst_ref=p_recv.at[m - 1],
            send_sem=ps_sem.at[m - 1],
            recv_sem=pr_sem.at[m - 1],
            device_id={"peer": toggled(me, 2 * m)},
            device_id_type=MESH,
        )
        for m in range(1, half)
    ]
    core_move.wait_recv()
    for d in reversed(range(groups)):
        theirs = pl.ds(pl.multiple_of(lax.rem(grp + d, groups) * gcols, gcols), gcols)
        for m in range(half):
            ours = pl.multiple_of(toggled(me, 2 * m) * part, part)
            pair = gfull_ref[pl.ds(ours, zpart), theirs]
            pair = pair + core_recv[pl.ds(m * part, zpart), theirs].astype(F32)
            mr = pl.ds(m * zpart, zpart)
            if d:
                z_send[d - 1, mr, :] = pair.astype(BF16)
            else:
                held_ref[mr, :] = pair
        if d:
            z_moves[d - 1].start()
    for m in reversed(range(half)):
        ours = pl.multiple_of(toggled(me, 2 * m) * part + zpart, qpart)
        pair = gfull_ref[pl.ds(ours, qpart), :]
        pair = pair + core_recv[pl.ds(m * part + zpart, qpart), :].astype(F32)
        if m:
            q_send[m - 1] = pair.astype(BF16)
            q_moves[m - 1].start()
        else:
            kept_ref[...] = pair
    backward(0)

    def unpack_grad(n, _):
        cols = pl.ds(pl.multiple_of(n * col, col), col)
        grad_ref[:, cols] = dotf(untake_ref[...], gradp_ref[:, cols]).astype(BF16)
        return 0

    lax.fori_loop(0, width // col, unpack_grad, 0, unroll=True)

    for j in range(1, peers):
        out_moves[j].wait_recv()

    def unpack_out(n, _):
        cols = pl.ds(pl.multiple_of(n * col, col), col)
        out_ref[:, cols] = dotf(unpack_ref[...], orecv[:, cols]).astype(BF16)
        return 0

    lax.fori_loop(0, width // col, unpack_out, 0, unroll=True)

    grad_scale = 1.0 / math.sqrt(groups * peers * work_rows)
    share = held_ref[pl.ds(0, zpart), :]
    for m in range(1, half):
        p_moves[m - 1].wait_recv()
        share = share + p_recv[m - 1].astype(F32)
    gproj_ref[pl.ds(0, zpart), :] = share * grad_scale
    share = kept_ref[:, pl.ds(pl.multiple_of(grp * gcols, gcols), gcols)]
    for d in range(1, groups):
        r_moves[d - 1].wait_recv()
        share = share + r_recv[d - 1].astype(F32)
    gproj_ref[pl.ds(zpart, qpart), :] = share * grad_scale

    for j in range(1, peers):
        cot_moves[j].wait_send()
        out_moves[j].wait_send()
    core_move.wait_send()
    for move in z_moves + p_moves + q_moves + r_moves:
        move.wait_send()


def fused_shards(embed, lengths, w_in, w_out, cotangent):
    peers = lax.axis_size("peer")
    groups = lax.axis_size("group")
    rows, width = embed.shape
    work_rows = cotangent.shape[0]
    attn = w_out.shape[0]
    tile = rows
    sub = min(tile, 128)
    heads = attn // HD
    part = attn // peers
    gcols = width // groups
    half = peers // 2
    vmem = pltpu.VMEM
    dma = pltpu.SemaphoreType.DMA
    scratch = [
        vmem(lengths.shape, jnp.int32),
        vmem((work_rows, width), BF16),
        vmem((rows, width), BF16),
        vmem(w_in.shape, BF16),
        vmem(w_out.shape, BF16),
        vmem((rows, width), BF16),
        vmem((rows, width), BF16),
        vmem((rows, width), BF16),
        vmem((rows, width), BF16),
        vmem((rows, rows), BF16),
        vmem((rows, work_rows), BF16),
        vmem((work_rows, rows), BF16),
        vmem((rows, rows), BF16),
        vmem((attn, rows), BF16),
        vmem((rows, width), BF16),
        vmem((rows, width), BF16),
        vmem((rows, 1), F32),
        vmem((rows, 4 * attn), BF16),
        vmem((rows, 4 * attn), BF16),
        vmem((rows, heads * sub), BF16),
        vmem((rows, heads * sub), BF16),
        vmem((rows, attn), BF16),
        vmem((rows, attn), BF16),
        vmem((rows, 1), F32),
        vmem((rows, 1), F32),
        vmem((rows, 1), F32),
        vmem((tile, attn), BF16),
        vmem((tile, 4 * attn), BF16),
        vmem((tile, width), BF16),
        vmem((rows, width), BF16),
        vmem((attn, width), F32),
        vmem((half * part, width), BF16),
        vmem((half * part, width), BF16),
        vmem((half * (part // 2), gcols), F32),
        vmem((part - part // 2, width), F32),
        vmem((groups - 1, half * (part // 2), gcols), BF16),
        vmem((groups - 1, half * (part // 2), gcols), BF16),
        vmem((half - 1, part // 2, gcols), BF16),
        vmem((half - 1, part // 2, gcols), BF16),
        vmem((half - 1, part - part // 2, width), BF16),
        vmem((half - 1, part - part // 2, width), BF16),
        vmem((groups - 1, part - part // 2, gcols), BF16),
        vmem((groups - 1, part - part // 2, gcols), BF16),
        dma((5,)),
        dma((peers,)),
        dma((peers,)),
        dma((peers,)),
        dma((peers,)),
        dma((2,)),
        dma((groups - 1,)),
        dma((groups - 1,)),
        dma((half - 1,)),
        dma((half - 1,)),
        dma((half - 1,)),
        dma((half - 1,)),
        dma((groups - 1,)),
        dma((groups - 1,)),
    ]
    pinned = pl.BlockSpec(memory_space=pltpu.HBM)
    resident = pl.BlockSpec(memory_space=pltpu.VMEM)
    return pl.pallas_call(
        functools.partial(fused, peers, groups),
        out_shape=(
            jax.ShapeDtypeStruct((work_rows, width), BF16),
            jax.ShapeDtypeStruct((rows, width), BF16),
            jax.ShapeDtypeStruct((part, gcols), F32),
        ),
        in_specs=[pinned] * 5,
        out_specs=(resident, resident, resident),
        scratch_shapes=scratch,
        compiler_params=pltpu.CompilerParams(
            collective_id=0, has_side_effects=True, vmem_limit_bytes=54_000_000
        ),
        cost_estimate=pl.CostEstimate(
            flops=2 * rows * width * attn * 11,
            bytes_accessed=2 * (w_in.size + w_out.size + 3 * rows * width),
            transcendentals=rows * attn * 5,
        ),
    )(lengths, embed, w_in, w_out, cotangent)


def fits(mesh):
    peers = mesh.shape["peer"]

    def check(embed, lengths, w_out):
        rows = embed.shape[0] // (peers * mesh.shape["group"])
        part, left = divmod(w_out.shape[0], peers)
        return (
            peers & (peers - 1) == 0
            and peers >= 4
            and mesh.shape["group"] > 1
            and rows % (16 * peers) == 0
            and rows % 256 == 0
            and 256 % (rows // peers) == 0
            and left == 0
            and part % 32 == 0
            and embed.shape[1] % (256 * mesh.shape["group"]) == 0
            and lengths.shape[1] * BLK == rows * peers
        )

    return check


def solution(mesh):
    placed = (P(("group", "peer"), None), P("group", None), P(), P(), P(("group", "peer"), None))

    def mapped(body):
        return jax.shard_map(
            body,
            mesh=mesh,
            in_specs=placed,
            out_specs=(P(("group", "peer"), None), P(("group", "peer"), None), P("peer", "group")),
            check_vma=False,
        )

    def run(embed, lengths, w_in, w_out, cotangent):
        body = fused_shards if fits(mesh)(embed, lengths, w_out) else shards
        return mapped(body)(embed, lengths, w_in, w_out, cotangent)

    return run
```

```python
import functools
import math

import jax
import jax.numpy as jnp
from jax import lax
from jax.experimental import pallas as pl
from jax.experimental.pallas import tpu as pltpu
from jax.sharding import PartitionSpec as P

HD = 128
BLK = 8


EPSILON = 1e-06
MIX_FLOOR = 1.0


def shortened(shard):

    def short(part):
        return part.astype(jnp.bfloat16) if part.dtype == jnp.float32 else part

    return jax.tree.map(short, shard)


def plan_tables(block_lengths):
    block_total = block_lengths.shape[1]
    is_live = (block_lengths > 0).astype(jnp.int32)
    counts = jnp.sum(is_live, axis=1)
    prefix = jnp.cumsum(counts) - counts
    block_rank = jnp.cumsum(is_live, axis=1) - is_live
    slot_index = jnp.arange(block_total, dtype=jnp.int32)
    chosen = (block_rank[:, :, None] == slot_index[None, None, :]) & (is_live[:, :, None] > 0)
    chosen_int = chosen.astype(jnp.int32)
    block_of = jnp.sum(chosen_int * slot_index[None, :, None], axis=1)
    length_of = jnp.sum(chosen_int * block_lengths[:, :, None], axis=1)
    return (counts, prefix, block_rank, block_of, length_of)


def layer(inputs, work_len, w_in, w_out):
    block_count = inputs.shape[0]
    block_len = inputs.shape[1]
    model_width = inputs.shape[2]
    attn_width = w_out.shape[0]
    head_count = attn_width // HD
    floated = inputs.astype(jnp.float32)
    row_mean = jnp.mean(floated, axis=-1, keepdims=True)
    centred = floated - row_mean
    row_var = jnp.mean(centred * centred, axis=-1, keepdims=True)
    normed = (centred * lax.rsqrt(row_var + EPSILON)).astype(jnp.bfloat16)
    projected = jnp.dot(normed.reshape(-1, model_width), w_in, preferred_element_type=jnp.float32)
    activated = jax.nn.silu(projected).astype(jnp.bfloat16)
    gating = activated[:, :attn_width]
    values = activated[:, attn_width : 2 * attn_width].reshape(
        block_count, block_len, head_count, HD
    )
    queries = activated[:, 2 * attn_width : 3 * attn_width].reshape(
        block_count, block_len, head_count, HD
    )
    key_rows = activated[:, 3 * attn_width :].reshape(block_count, block_len, head_count, HD)
    scores = jnp.einsum(
        "bihd,bjhd->bhij", queries.astype(jnp.float32), key_rows.astype(jnp.float32)
    ) * HD ** (-0.5)
    position = jnp.arange(block_len, dtype=jnp.int32)
    causal = position[None, :] <= position[:, None]
    limit = work_len[:, None, None, None]
    allowed = (
        causal[None, None, :, :]
        & (position[None, None, None, :] < limit)
        & (position[None, None, :, None] < limit)
    )
    weights = jnp.where(allowed, jax.nn.silu(scores), 0.0).astype(jnp.bfloat16)
    mixed = jnp.einsum("bhij,bjhd->bihd", weights.astype(jnp.float32), values.astype(jnp.float32))
    mixed = mixed.reshape(block_count * block_len, attn_width)
    mix_mean = jnp.mean(mixed, axis=-1, keepdims=True)
    mix_centred = mixed - mix_mean
    mix_var = jnp.mean(mix_centred * mix_centred, axis=-1, keepdims=True)
    gated = (
        mix_centred * lax.rsqrt(jnp.maximum(mix_var, MIX_FLOOR)) * gating.astype(jnp.float32)
    ).astype(jnp.bfloat16)
    output = floated.reshape(-1, model_width) + jnp.dot(
        gated, w_out, preferred_element_type=jnp.float32
    )
    rows_ok = (position[None, :] < work_len[:, None]).reshape(-1, 1)
    result = (
        jnp.where(rows_ok, output, 0.0)
        .astype(jnp.bfloat16)
        .reshape(block_count, block_len, model_width)
    )
    return (result, gated)


def shards(embed, lengths, w_in, w_out, cotangent):
    peer_count = lax.axis_size("peer")
    group_total = lax.axis_size("group")
    own_peer = lax.axis_index("peer")
    model_width = embed.shape[1]
    blocks = lengths.shape[1] // peer_count
    pair_depth = (blocks + peer_count - 1) // peer_count
    work_slots = cotangent.shape[0] // BLK
    block_lengths = lengths[0].reshape(peer_count, blocks)
    counts, prefix, block_rank, block_of, length_of = plan_tables(block_lengths)
    own_prefix = prefix[own_peer]
    own_count = counts[own_peer]
    dest_index = jnp.arange(peer_count, dtype=jnp.int32)
    pair_index = jnp.arange(pair_depth, dtype=jnp.int32)
    offset = ((dest_index - own_prefix) % peer_count)[:, None] + pair_index[None, :] * peer_count
    is_valid = offset < own_count
    picked = block_of[own_peer][jnp.minimum(offset, blocks - 1)]
    home_rows = embed.reshape(blocks, BLK, model_width)
    outgoing = jnp.where(is_valid[:, :, None, None], home_rows[picked], jnp.zeros((), embed.dtype))
    arrived = lax.all_to_all(
        outgoing.reshape(peer_count, pair_depth * BLK, model_width),
        "peer",
        split_axis=0,
        concat_axis=0,
        tiled=True,
    )
    arrived = arrived.reshape(peer_count, pair_depth, BLK, model_width)
    ticket = jnp.arange(work_slots, dtype=jnp.int32) * peer_count + own_peer
    source_end = prefix + counts
    source = jnp.sum((source_end[None, :] <= ticket[:, None]).astype(jnp.int32), axis=1)
    source = jnp.minimum(source, peer_count - 1)
    within = jnp.clip(ticket - prefix[source], 0, blocks - 1)
    work_len = length_of[source, within]
    work_rows = arrived[source, jnp.minimum(within // peer_count, pair_depth - 1)]
    result, pullback, gated = jax.vjp(
        lambda inputs: layer(inputs, work_len, w_in, w_out), work_rows, has_aux=True
    )
    cotan_blocks = cotangent.reshape(work_slots, BLK, model_width)
    (grad_work,) = pullback(cotan_blocks)
    back_offset = ((own_peer - prefix) % peer_count)[:, None] + pair_index[None, :] * peer_count
    back_valid = back_offset < counts[:, None]
    back_slot = jnp.clip((prefix[:, None] + back_offset) // peer_count, 0, work_slots - 1)
    returning = jnp.where(
        back_valid[:, :, None, None], grad_work[back_slot], jnp.zeros((), grad_work.dtype)
    )
    returned = lax.all_to_all(
        shortened(returning.reshape(peer_count, pair_depth * BLK, model_width)),
        "peer",
        split_axis=0,
        concat_axis=0,
        tiled=True,
    )
    returned = returned.reshape(peer_count, pair_depth, BLK, model_width)
    own_rank = block_rank[own_peer]
    target = (own_prefix + own_rank) % peer_count
    own_live = block_lengths[own_peer] > 0
    grad_back = jnp.where(
        own_live[:, None, None],
        returned[target, jnp.minimum(own_rank // peer_count, pair_depth - 1)],
        jnp.zeros((), returned.dtype),
    )
    attn_width = w_out.shape[0]
    grad_scale = 1.0 / math.sqrt(group_total * peer_count * work_slots * BLK)
    columns = lax.slice_in_dim(gated, 0, attn_width // peer_count * lax.axis_size("peer"), axis=1)
    grad_share = lax.psum_scatter(
        lax.dot_general(
            columns, cotangent, (((0,), (0,)), ((), ())), preferred_element_type=jnp.float32
        )
        * grad_scale,
        "peer",
        scatter_dimension=0,
        tiled=True,
    )
    grad_piece = lax.psum_scatter(grad_share, "group", scatter_dimension=1, tiled=True)
    return (result.reshape(-1, model_width), grad_back.reshape(-1, model_width), grad_piece)


MESH = pl.DeviceIdType.MESH
F32 = jnp.float32
BF16 = jnp.bfloat16
NT = (((1,), (1,)), ((), ()))
TN = (((0,), (0,)), ((), ()))


def toggled(index, bits):
    result = index
    bit = 1
    while bit <= bits:
        if bits & bit:
            result = result + bit * (1 - 2 * lax.rem(lax.div(index, bit), 2))
        bit *= 2
    return result


def dotf(a, b, dims=None):
    if dims is None:
        return jnp.dot(a, b, preferred_element_type=F32)
    return lax.dot_general(a, b, dims, preferred_element_type=F32)


def fused(
    peers,
    groups,
    len_hbm,
    embed_hbm,
    w_in_hbm,
    w_out_hbm,
    cot_hbm,
    out_ref,
    grad_ref,
    gproj_ref,
    len_ref,
    cot_v,
    embed_v,
    w_in_v,
    w_out_v,
    csend,
    crecv,
    osend,
    orecv,
    take_ref,
    pack_ref,
    unpack_ref,
    untake_ref,
    gated_t_ref,
    x_ref,
    nrm_ref,
    inv_ref,
    act_ref,
    der_ref,
    wts_ref,
    dsw_ref,
    y_ref,
    gated_ref,
    inv2_ref,
    flag_ref,
    valid_ref,
    dg_ref,
    dproj_ref,
    dn_ref,
    gradp_ref,
    gfull_ref,
    core_send,
    core_recv,
    held_ref,
    kept_ref,
    z_send,
    z_recv,
    p_send,
    p_recv,
    q_send,
    q_recv,
    r_send,
    r_recv,
    in_sem,
    cs_sem,
    cr_sem,
    os_sem,
    or_sem,
    core_sem,
    zs_sem,
    zr_sem,
    ps_sem,
    pr_sem,
    qs_sem,
    qr_sem,
    rs_sem,
    rr_sem,
):
    me = lax.axis_index("peer")
    grp = lax.axis_index("group")
    rows, width = embed_v.shape
    work_rows = cot_v.shape[0]
    attn = w_out_v.shape[0]
    heads = attn // HD
    chunk = rows // peers
    blocks = rows // BLK
    total = len_ref.shape[1]
    tile = min(rows, 256)
    tiles = rows // tile
    bit_count = peers.bit_length() - 1
    col = 256
    part = attn // peers
    gcols = width // groups
    half = peers // 2
    zpart = part // 2
    qpart = part - zpart

    len_load = pltpu.make_async_copy(len_hbm, len_ref, in_sem.at[4])
    len_load.start()
    loads = []
    for place, (src, dst) in enumerate(
        (
            (cot_hbm, cot_v),
            (embed_hbm, embed_v),
            (w_in_hbm, w_in_v),
            (w_out_hbm, w_out_v),
        )
    ):
        load = pltpu.make_async_copy(src, dst, in_sem.at[place])
        load.start()
        loads.append(load)

    barrier = pltpu.get_barrier_semaphore()
    for j in range(1, peers):
        pl.semaphore_signal(
            barrier, inc=1, device_id={"peer": toggled(me, j)}, device_id_type=MESH
        )
    for d in range(1, groups):
        pl.semaphore_signal(
            barrier, inc=1, device_id={"group": lax.rem(grp + d, groups)}, device_id_type=MESH
        )

    len_load.wait()
    lens = len_ref[...]
    live = jnp.where(lens > 0, 1.0, 0.0).astype(F32)
    lane = lax.broadcasted_iota(jnp.int32, (1, total), 1)
    before = (
        lax.broadcasted_iota(jnp.int32, (total, total), 0)
        < lax.broadcasted_iota(jnp.int32, (total, total), 1)
    )
    before = jnp.where(before, 1.0, 0.0).astype(BF16)
    ticket = dotf(jnp.broadcast_to(live, (16, total)).astype(BF16), before).astype(jnp.int32)
    peer_end = (
        lax.broadcasted_iota(jnp.int32, (peers, total), 1)
        < (lax.broadcasted_iota(jnp.int32, (peers, total), 0) + 1) * blocks
    )
    ends = jnp.sum(jnp.where(peer_end, live, 0.0), axis=1, keepdims=True).astype(jnp.int32)
    own_prefix = jnp.sum(jnp.where(lane < me * blocks, live, 0.0), axis=1, keepdims=True).astype(
        jnp.int32
    )

    wlane = lax.broadcasted_iota(jnp.int32, (1, work_rows), 1)
    wticket = lax.shift_right_logical(wlane, 3) * peers + me
    passed = ends <= wticket
    source = jnp.sum(jnp.where(passed, 1, 0), axis=0, keepdims=True)
    start = jnp.max(jnp.where(passed, ends, 0), axis=0, keepdims=True)
    depth = lax.shift_right_logical(wticket - start, bit_count)
    wtarget = (source ^ me) * chunk + depth * BLK + (wlane & (BLK - 1))
    pack_ref[...] = jnp.where(
        lax.broadcasted_iota(jnp.int32, (rows, work_rows), 0) == wtarget, 1.0, 0.0
    ).astype(BF16)

    loads[0].wait()

    def exchange(src, dst, s_sem, r_sem, j):
        span = pl.ds(j * chunk, chunk)
        return pltpu.make_async_remote_copy(
            src_ref=src.at[span],
            dst_ref=dst.at[span],
            send_sem=s_sem.at[j],
            recv_sem=r_sem.at[j],
            device_id={"peer": toggled(me, j)},
            device_id_type=MESH,
        )

    cot_moves = {j: exchange(csend, crecv, cs_sem, cr_sem, j) for j in range(1, peers)}
    for u in reversed(range(half)):
        duo = pl.ds(u * 2 * chunk, 2 * chunk)
        csend[duo, :] = dotf(pack_ref[duo, :], cot_v[...]).astype(BF16)
        if u == half - 1:
            pl.semaphore_wait(barrier, peers - 1 + groups - 1)
        for j in (2 * u + 1, 2 * u):
            if j:
                cot_moves[j].start()
    crecv[pl.ds(0, chunk), :] = csend[pl.ds(0, chunk), :]

    spot = lax.broadcasted_iota(jnp.int32, (16, total), 0)
    high = lax.shift_right_logical(ticket, 7)
    low = ticket & 127
    facts = jnp.where(spot == 0, high, jnp.where(spot == 1, low, lens)).astype(F32).astype(BF16)
    spread = (
        lax.broadcasted_iota(jnp.int32, (total, rows), 0)
        == me * blocks + lax.shift_right_logical(lax.broadcasted_iota(jnp.int32, (total, rows), 1), 3)
    )
    facts = dotf(facts, jnp.where(spread, 1.0, 0.0).astype(BF16)).astype(jnp.int32)
    hticket = facts[0:1] * 128 + facts[1:2]
    hlen = facts[2:3]
    hlane = lax.broadcasted_iota(jnp.int32, (1, rows), 1)
    rank = hticket - own_prefix
    target = (
        ((hticket & (peers - 1)) ^ me) * chunk
        + lax.shift_right_logical(rank, bit_count) * BLK
        + (hlane & (BLK - 1))
    )
    target = jnp.where(hlen > 0, target, -1)
    chosen = lax.broadcasted_iota(jnp.int32, (rows, rows), 0) == target
    take_ref[...] = jnp.where(chosen, 1.0, 0.0).astype(BF16)
    slot_len = jnp.sum(
        jnp.where(chosen, hlen.astype(F32), 0.0), axis=1, keepdims=True
    )
    row_in = lax.broadcasted_iota(jnp.int32, (rows, 1), 0) & (BLK - 1)
    valid_ref[...] = jnp.where(row_in.astype(F32) < slot_len, 1.0, 0.0)

    def upright(line):
        return jnp.transpose(jnp.broadcast_to(line.astype(F32), (128, line.shape[1])))[:, 0:1]

    slots = lax.broadcasted_iota(jnp.int32, (1, rows), 1).astype(F32)
    untake_ref[...] = jnp.where(upright(target) == slots, 1.0, 0.0).astype(BF16)
    unpack_ref[...] = jnp.where(upright(wtarget) == slots, 1.0, 0.0).astype(BF16)

    out_moves = {j: exchange(osend, orecv, os_sem, or_sem, j) for j in range(1, peers)}
    small = 64
    scale = HD ** (-0.5)
    sub = min(tile, 128)
    si = lax.broadcasted_iota(jnp.int32, (sub, sub), 0)
    sj = lax.broadcasted_iota(jnp.int32, (sub, sub), 1)
    near = (lax.shift_right_logical(si, 3) == lax.shift_right_logical(sj, 3)) & (sj <= si)
    near = jnp.where(near, 1.0, 0.0)

    loads[1].wait()
    for place, t in enumerate(reversed(range(tiles))):
        span = pl.ds(t * tile, tile)

        def pick(n, _):
            cols = pl.ds(pl.multiple_of(n * col, col), col)
            x_ref[span, cols] = dotf(take_ref[span, :], embed_v[:, cols]).astype(BF16)
            return 0

        lax.fori_loop(0, width // col, pick, 0, unroll=True)

        def norm(s, _):
            part_rows = pl.ds(pl.multiple_of(t * tile + s * small, small), small)
            x = x_ref[part_rows, :].astype(F32)
            x = x - jnp.mean(x, axis=1, keepdims=True)
            inv = lax.rsqrt(jnp.mean(x * x, axis=1, keepdims=True) + EPSILON)
            nrm_ref[part_rows, :] = (x * inv).astype(BF16)
            inv_ref[part_rows, :] = inv
            return 0

        lax.fori_loop(0, tile // small, norm, 0, unroll=True)
        if place == 0:
            loads[2].wait()

        def project(n, _):
            cols = pl.ds(pl.multiple_of(n * col, col), col)
            v = dotf(nrm_ref[span, :], w_in_v[:, cols])
            sig = 0.5 * jnp.tanh(0.5 * v) + 0.5
            act = v * sig
            act_ref[span, cols] = act.astype(BF16)
            der_ref[span, cols] = (sig + act * (1.0 - sig)).astype(BF16)
            return 0

        lax.fori_loop(0, 4 * attn // col, project, 0, unroll=True)

        def attend(s, _):
            sr = pl.ds(pl.multiple_of(t * tile + s * sub, sub), sub)
            allowed = near * valid_ref[sr, :]
            mixed = []
            for h in range(heads):
                hc = pl.ds(h * HD, HD)
                values = act_ref[sr, pl.ds(attn + h * HD, HD)]
                queries = act_ref[sr, pl.ds(2 * attn + h * HD, HD)]
                keys = act_ref[sr, pl.ds(3 * attn + h * HD, HD)]
                score = dotf(queries, keys, NT) * scale
                sig = 0.5 * jnp.tanh(0.5 * score) + 0.5
                weight = score * sig
                slope = (sig + weight * (1.0 - sig)) * scale
                weight = jnp.where(allowed > 0.0, weight, 0.0).astype(BF16)
                wts_ref[sr, pl.ds(h * sub, sub)] = weight
                dsw_ref[sr, pl.ds(h * sub, sub)] = jnp.where(allowed > 0.0, slope, 0.0).astype(BF16)
                mixed.append(dotf(weight, values))
            mixed = jnp.concatenate(mixed, axis=1)
            mixed = mixed - jnp.mean(mixed, axis=1, keepdims=True)
            var = jnp.mean(mixed * mixed, axis=1, keepdims=True)
            inv = lax.rsqrt(jnp.maximum(var, MIX_FLOOR))
            y = mixed * inv
            inv2_ref[sr, :] = inv
            flag_ref[sr, :] = jnp.where(
                var > MIX_FLOOR, 1.0, jnp.where(var == MIX_FLOOR, 0.5, 0.0)
            )
            y_ref[sr, :] = y.astype(BF16)
            gated = y * act_ref[sr, pl.ds(0, attn)].astype(F32)
            gated_ref[sr, :] = gated.astype(BF16)
            gated_t_ref[:, sr] = jnp.transpose(gated).astype(BF16)
            return 0

        lax.fori_loop(0, tile // sub, attend, 0, unroll=True)
        if place == 0:
            loads[3].wait()

        def produce(n, _):
            cols = pl.ds(pl.multiple_of(n * col, col), col)
            out = x_ref[span, cols].astype(F32) + dotf(gated_ref[span, :], w_out_v[:, cols])
            osend[span, cols] = jnp.where(valid_ref[span, :] > 0.0, out, 0.0).astype(BF16)
            return 0

        lax.fori_loop(0, width // col, produce, 0, unroll=True)
        for j in reversed(range(t * tile // chunk, (t + 1) * tile // chunk)):
            if j:
                out_moves[j].start()
    orecv[pl.ds(0, chunk), :] = osend[pl.ds(0, chunk), :]

    for j in range(1, peers):
        cot_moves[j].wait_recv()

    def outer(n, _):
        cols = pl.ds(pl.multiple_of(n * col, col), col)
        gfull_ref[:, cols] = dotf(gated_t_ref[...], crecv[:, cols])
        return 0

    lax.fori_loop(0, width // col, outer, 0, unroll=True)
    for m in range(half):
        theirs = pl.multiple_of(toggled(me, 2 * m + 1) * part, part)
        core_send[pl.ds(m * part, part), :] = gfull_ref[pl.ds(theirs, part), :].astype(BF16)
    core_move = pltpu.make_async_remote_copy(
        src_ref=core_send,
        dst_ref=core_recv,
        send_sem=core_sem.at[0],
        recv_sem=core_sem.at[1],
        device_id={"peer": toggled(me, 1)},
        device_id_type=MESH,
    )
    core_move.start()

    def back_out(n, _):
        cols = pl.ds(pl.multiple_of(n * col, col), col)
        dg_ref[:, cols] = dotf(crecv[...], w_out_v[cols, :], NT).astype(BF16)
        return 0

    lax.fori_loop(0, attn // col, back_out, 0, unroll=True)

    def backward():
        def back_attend(s, _):
            here = pl.ds(pl.multiple_of(s * sub, sub), sub)
            sr = pl.ds(pl.multiple_of(s * sub, sub), sub)
            dg = dg_ref[here, :].astype(F32) * valid_ref[sr, :]
            y = y_ref[sr, :].astype(F32)
            gate = pl.ds(0, attn)
            dgate = (dg * y).astype(BF16).astype(F32)
            dproj_ref[here, gate] = (dgate * der_ref[sr, gate].astype(F32)).astype(BF16)
            dy = dg * act_ref[sr, gate].astype(F32)
            slant = jnp.mean(dy * y, axis=1, keepdims=True) * flag_ref[sr, :]
            dc = (dy - y * slant) * inv2_ref[sr, :]
            dmix = (dc - jnp.mean(dc, axis=1, keepdims=True)).astype(BF16)
            for h in range(heads):
                vc = pl.ds(attn + h * HD, HD)
                qc = pl.ds(2 * attn + h * HD, HD)
                kc = pl.ds(3 * attn + h * HD, HD)
                dm = dmix[:, h * HD : (h + 1) * HD]
                dw = dotf(dm, act_ref[sr, vc], NT).astype(BF16).astype(F32)
                ds = (dw * dsw_ref[sr, pl.ds(h * sub, sub)].astype(F32)).astype(BF16)
                dv = dotf(wts_ref[sr, pl.ds(h * sub, sub)], dm, TN)
                dq = dotf(ds, act_ref[sr, kc])
                dk = dotf(ds, act_ref[sr, qc], TN)
                for place_of, grad in ((vc, dv), (qc, dq), (kc, dk)):
                    grad = grad.astype(BF16).astype(F32)
                    dproj_ref[here, place_of] = (grad * der_ref[sr, place_of].astype(F32)).astype(BF16)
            return 0

        lax.fori_loop(0, rows // sub, back_attend, 0, unroll=True)

        def back_in(n, _):
            cols = pl.ds(pl.multiple_of(n * col, col), col)
            dn_ref[:, cols] = dotf(dproj_ref[...], w_in_v[cols, :], NT).astype(BF16)
            return 0

        lax.fori_loop(0, width // col, back_in, 0, unroll=True)

        for move in q_moves:
            move.wait_recv()
        mine = pl.ds(pl.multiple_of(grp * gcols, gcols), gcols)
        for d in reversed(range(groups)):
            theirs = pl.ds(pl.multiple_of(lax.rem(grp + d, groups) * gcols, gcols), gcols)
            share = kept_ref[:, theirs]
            for m in range(1, half):
                share = share + q_recv[m - 1, :, theirs].astype(F32)
            if d:
                r_send[d - 1] = share.astype(BF16)
                r_moves[d - 1].start()
            else:
                kept_ref[:, mine] = share

        for move in z_moves:
            move.wait_recv()
        for m in reversed(range(half)):
            mr = pl.ds(m * zpart, zpart)
            share = held_ref[mr, :]
            for d in range(1, groups):
                share = share + z_recv[d - 1, mr, :].astype(F32)
            if m:
                p_send[m - 1] = share.astype(BF16)
                p_moves[m - 1].start()
            else:
                held_ref[mr, :] = share

        def back_norm(s, _):
            here = pl.ds(pl.multiple_of(s * small, small), small)
            sr = pl.ds(pl.multiple_of(s * small, small), small)
            dn = dn_ref[here, :].astype(F32)
            xh = nrm_ref[sr, :].astype(F32)
            dc = (dn - xh * jnp.mean(dn * xh, axis=1, keepdims=True)) * inv_ref[sr, :]
            dx = dc - jnp.mean(dc, axis=1, keepdims=True)
            gradp_ref[sr, :] = (crecv[sr, :].astype(F32) * valid_ref[sr, :] + dx).astype(BF16)
            return 0

        lax.fori_loop(0, rows // small, back_norm, 0, unroll=True)

    z_moves = [
        pltpu.make_async_remote_copy(
            src_ref=z_send.at[d - 1],
            dst_ref=z_recv.at[d - 1],
            send_sem=zs_sem.at[d - 1],
            recv_sem=zr_sem.at[d - 1],
            device_id={"group": lax.rem(grp + d, groups)},
            device_id_type=MESH,
        )
        for d in range(1, groups)
    ]
    r_moves = [
        pltpu.make_async_remote_copy(
            src_ref=r_send.at[d - 1],
            dst_ref=r_recv.at[d - 1],
            send_sem=rs_sem.at[d - 1],
            recv_sem=rr_sem.at[d - 1],
            device_id={"group": lax.rem(grp + d, groups)},
            device_id_type=MESH,
        )
        for d in range(1, groups)
    ]
    q_moves = [
        pltpu.make_async_remote_copy(
            src_ref=q_send.at[m - 1],
            dst_ref=q_recv.at[m - 1],
            send_sem=qs_sem.at[m - 1],
            recv_sem=qr_sem.at[m - 1],
            device_id={"peer": toggled(me, 2 * m)},
            device_id_type=MESH,
        )
        for m in range(1, half)
    ]
    p_moves = [
        pltpu.make_async_remote_copy(
            src_ref=p_send.at[m - 1],
            dst_ref=p_recv.at[m - 1],
            send_sem=ps_sem.at[m - 1],
            recv_sem=pr_sem.at[m - 1],
            device_id={"peer": toggled(me, 2 * m)},
            device_id_type=MESH,
        )
        for m in range(1, half)
    ]
    core_move.wait_recv()
    for d in reversed(range(groups)):
        theirs = pl.ds(pl.multiple_of(lax.rem(grp + d, groups) * gcols, gcols), gcols)
        for m in range(half):
            ours = pl.multiple_of(toggled(me, 2 * m) * part, part)
            pair = gfull_ref[pl.ds(ours, zpart), theirs]
            pair = pair + core_recv[pl.ds(m * part, zpart), theirs].astype(F32)
            mr = pl.ds(m * zpart, zpart)
            if d:
                z_send[d - 1, mr, :] = pair.astype(BF16)
            else:
                held_ref[mr, :] = pair
        if d:
            z_moves[d - 1].start()
    for m in reversed(range(half)):
        ours = pl.multiple_of(toggled(me, 2 * m) * part + zpart, qpart)
        pair = gfull_ref[pl.ds(ours, qpart), :]
        pair = pair + core_recv[pl.ds(m * part + zpart, qpart), :].astype(F32)
        if m:
            q_send[m - 1] = pair.astype(BF16)
            q_moves[m - 1].start()
        else:
            kept_ref[...] = pair
    backward()

    def unpack_grad(n, _):
        cols = pl.ds(pl.multiple_of(n * col, col), col)
        grad_ref[:, cols] = dotf(untake_ref[...], gradp_ref[:, cols]).astype(BF16)
        return 0

    lax.fori_loop(0, width // col, unpack_grad, 0, unroll=True)

    for j in range(1, peers):
        out_moves[j].wait_recv()

    def unpack_out(n, _):
        cols = pl.ds(pl.multiple_of(n * col, col), col)
        out_ref[:, cols] = dotf(unpack_ref[...], orecv[:, cols]).astype(BF16)
        return 0

    lax.fori_loop(0, width // col, unpack_out, 0, unroll=True)

    grad_scale = 1.0 / math.sqrt(groups * peers * work_rows)
    share = held_ref[pl.ds(0, zpart), :]
    for m in range(1, half):
        p_moves[m - 1].wait_recv()
        share = share + p_recv[m - 1].astype(F32)
    gproj_ref[pl.ds(0, zpart), :] = share * grad_scale
    share = kept_ref[:, pl.ds(pl.multiple_of(grp * gcols, gcols), gcols)]
    for d in range(1, groups):
        r_moves[d - 1].wait_recv()
        share = share + r_recv[d - 1].astype(F32)
    gproj_ref[pl.ds(zpart, qpart), :] = share * grad_scale

    for j in range(1, peers):
        cot_moves[j].wait_send()
        out_moves[j].wait_send()
    core_move.wait_send()
    for move in z_moves + p_moves + q_moves + r_moves:
        move.wait_send()


def fused_shards(embed, lengths, w_in, w_out, cotangent):
    peers = lax.axis_size("peer")
    groups = lax.axis_size("group")
    rows, width = embed.shape
    work_rows = cotangent.shape[0]
    attn = w_out.shape[0]
    tile = rows
    sub = min(tile, 128)
    heads = attn // HD
    part = attn // peers
    gcols = width // groups
    half = peers // 2
    vmem = pltpu.VMEM
    dma = pltpu.SemaphoreType.DMA
    scratch = [
        vmem(lengths.shape, jnp.int32),
        vmem((work_rows, width), BF16),
        vmem((rows, width), BF16),
        vmem(w_in.shape, BF16),
        vmem(w_out.shape, BF16),
        vmem((rows, width), BF16),
        vmem((rows, width), BF16),
        vmem((rows, width), BF16),
        vmem((rows, width), BF16),
        vmem((rows, rows), BF16),
        vmem((rows, work_rows), BF16),
        vmem((work_rows, rows), BF16),
        vmem((rows, rows), BF16),
        vmem((attn, rows), BF16),
        vmem((rows, width), BF16),
        vmem((rows, width), BF16),
        vmem((rows, 1), F32),
        vmem((rows, 4 * attn), BF16),
        vmem((rows, 4 * attn), BF16),
        vmem((rows, heads * sub), BF16),
        vmem((rows, heads * sub), BF16),
        vmem((rows, attn), BF16),
        vmem((rows, attn), BF16),
        vmem((rows, 1), F32),
        vmem((rows, 1), F32),
        vmem((rows, 1), F32),
        vmem((tile, attn), BF16),
        vmem((tile, 4 * attn), BF16),
        vmem((tile, width), BF16),
        vmem((rows, width), BF16),
        vmem((attn, width), F32),
        vmem((half * part, width), BF16),
        vmem((half * part, width), BF16),
        vmem((half * (part // 2), gcols), F32),
        vmem((part - part // 2, width), F32),
        vmem((groups - 1, half * (part // 2), gcols), BF16),
        vmem((groups - 1, half * (part // 2), gcols), BF16),
        vmem((half - 1, part // 2, gcols), BF16),
        vmem((half - 1, part // 2, gcols), BF16),
        vmem((half - 1, part - part // 2, width), BF16),
        vmem((half - 1, part - part // 2, width), BF16),
        vmem((groups - 1, part - part // 2, gcols), BF16),
        vmem((groups - 1, part - part // 2, gcols), BF16),
        dma((5,)),
        dma((peers,)),
        dma((peers,)),
        dma((peers,)),
        dma((peers,)),
        dma((2,)),
        dma((groups - 1,)),
        dma((groups - 1,)),
        dma((half - 1,)),
        dma((half - 1,)),
        dma((half - 1,)),
        dma((half - 1,)),
        dma((groups - 1,)),
        dma((groups - 1,)),
    ]
    pinned = pl.BlockSpec(memory_space=pltpu.HBM)
    resident = pl.BlockSpec(memory_space=pltpu.VMEM)
    return pl.pallas_call(
        functools.partial(fused, peers, groups),
        out_shape=(
            jax.ShapeDtypeStruct((work_rows, width), BF16),
            jax.ShapeDtypeStruct((rows, width), BF16),
            jax.ShapeDtypeStruct((part, gcols), F32),
        ),
        in_specs=[pinned] * 5,
        out_specs=(resident, resident, resident),
        scratch_shapes=scratch,
        compiler_params=pltpu.CompilerParams(
            collective_id=0, has_side_effects=True, vmem_limit_bytes=54_000_000
        ),
        cost_estimate=pl.CostEstimate(
            flops=2 * rows * width * attn * 11,
            bytes_accessed=2 * (w_in.size + w_out.size + 3 * rows * width),
            transcendentals=rows * attn * 5,
        ),
    )(lengths, embed, w_in, w_out, cotangent)


def fits(mesh):
    peers = mesh.shape["peer"]

    def check(embed, lengths, w_out):
        rows = embed.shape[0] // (peers * mesh.shape["group"])
        part, left = divmod(w_out.shape[0], peers)
        return (
            peers & (peers - 1) == 0
            and peers >= 4
            and mesh.shape["group"] > 1
            and rows % (16 * peers) == 0
            and rows % 256 == 0
            and 256 % (rows // peers) == 0
            and left == 0
            and part % 32 == 0
            and embed.shape[1] % (256 * mesh.shape["group"]) == 0
            and lengths.shape[1] * BLK == rows * peers
        )

    return check


def solution(mesh):
    placed = (P(("group", "peer"), None), P("group", None), P(), P(), P(("group", "peer"), None))

    def mapped(body):
        return jax.shard_map(
            body,
            mesh=mesh,
            in_specs=placed,
            out_specs=(P(("group", "peer"), None), P(("group", "peer"), None), P("peer", "group")),
            check_vma=False,
        )

    def run(embed, lengths, w_in, w_out, cotangent):
        body = fused_shards if fits(mesh)(embed, lengths, w_out) else shards
        return mapped(body)(embed, lengths, w_in, w_out, cotangent)

    return run
```
